128 devices in a mesh: slab: 8 (over y_lo, z), energy: 16 (over x, y_hi, core).
Axes of the slice: x: 4, y: 4 (y_hi: 2, y_lo: 2; y = y_hi * 2 + y_lo), z: 4, core: 2. Of those that a mesh axis runs over, the one named last changes fastest.
Arguments:
- green_ret: bfloat16 [8, 16, 2, 1536, 1536], P('slab', 'energy'), may hold values from -2.5 to 2.5
- prev_lesser: float32 [8, 16, 2, 1536, 128], P('slab', 'energy'), may hold values from -8 to 8
- coupling_index: int32 [8, 3, 2], P('slab'), may hold values from 0 to 1, as said below
- coupling_values: float32 [8, 3, 128, 128], P('slab'), may hold values from -1.5 to 1.5
- phonon_shift: int32 [3], replicated, may hold values from 1 to 8, as said below
- phonon_weight: float32 [2, 3], replicated, may hold values from 0.1 to 0.5
Outputs:
- retarded_blocks: float32 [8, 16, 2, 1536, 128], P('slab', 'energy')
- lesser_blocks: float32 [8, 16, 2, 1536, 128], P('slab', 'energy')
The draws below stay inside these ranges and needn't reach their ends.
Inputs may be any that keep to these rules, and one draw needn't show every extreme that they name: `coupling_index`: within one slab the 3 block positions are distinct: each of the 2 diagonal blocks once and one block off the diagonal, in drawn order. `phonon_shift`: the 3 shifts are distinct; one of them is 1 and one is 8.
All inputs are finite; a program needn't handle non-finite values.
Results may differ from the reference program's by a relative error of at most 0.0052.
Values sent between devices are 32-bit elements; how exact they have to be, the bound alone decides.
A program may use at most 192 MiB of HBM per device.

```python
import math
import jax
import jax.numpy as jnp
from jax import lax

SLAB_ORBITALS = 1536
BW = 256
BLK = 128
NMODE = 3
SLAB_TOTAL = 8
ENERGY_POINTS = 16
NBLK = 12
NBW = 2
NNZ = 3


def channel_extent(key, sluggish_mask, sudden_spike):
    split_keys = jax.random.split(key, 3)
    stable_variant = jnp.exp(jax.random.uniform(split_keys[0], (1, ENERGY_POINTS, SLAB_ORBITALS), jnp.float32, math.log(0.88), math.log(0.96)))
    random_wobble = jnp.exp(jax.random.uniform(split_keys[1], (SLAB_TOTAL, ENERGY_POINTS, SLAB_ORBITALS), jnp.float32, math.log(0.96), 0.0))
    fast_variant = jnp.exp(jax.random.uniform(split_keys[2], (SLAB_TOTAL, ENERGY_POINTS, SLAB_ORBITALS), jnp.float32, math.log(0.3), math.log(0.6)))
    return jnp.where(sluggish_mask, stable_variant * random_wobble, fast_variant) * sudden_spike


def draw_green_ret(key, part):
    key = jax.random.fold_in(key, 11)
    split_keys = jax.random.split(key, 10)
    array_shape = (SLAB_TOTAL, ENERGY_POINTS, 2, SLAB_ORBITALS, SLAB_ORBITALS)
    noise_part = jnp.clip(jax.random.normal(split_keys[0], array_shape, jnp.float32), -6.0, 6.0)
    slow_share = 0.5
    row_index = jnp.arange(SLAB_ORBITALS, dtype=jnp.int32)[:, None]
    column_index = jnp.arange(SLAB_ORBITALS, dtype=jnp.int32)[None, :]
    on_diagonal = row_index == column_index
    right_left = (row_index >= SLAB_ORBITALS - BW) & (column_index == row_index - (SLAB_ORBITALS - BW))
    left_right = (column_index >= SLAB_ORBITALS - BW) & (row_index == column_index - (SLAB_ORBITALS - BW))
    corner_region = (row_index >= SLAB_ORBITALS - BW) & (column_index < BW) | (row_index < BW) & (column_index >= SLAB_ORBITALS - BW)
    noise_scale = jnp.where(corner_region, 0.36, 0.6) / math.sqrt(SLAB_ORBITALS)
    vector_shape = (SLAB_TOTAL, ENERGY_POINTS, SLAB_ORBITALS)
    broadening = jnp.exp(jax.random.uniform(split_keys[1], vector_shape, jnp.float32, math.log(0.3), math.log(1.5)))
    level_shift = jax.random.uniform(split_keys[2], vector_shape, jnp.float32, -0.5, 0.5)
    sluggish_mask = jax.random.uniform(split_keys[3], (1, ENERGY_POINTS, SLAB_ORBITALS), jnp.float32) < slow_share
    spike_slab = jax.random.randint(split_keys[4], (1, ENERGY_POINTS, 1), 0, SLAB_TOTAL)
    spike_depth = jnp.exp(jax.random.uniform(split_keys[5], (1, ENERGY_POINTS, SLAB_ORBITALS), jnp.float32, math.log(0.7), math.log(0.9)))
    sudden_spike = jnp.where(jnp.arange(SLAB_TOTAL, dtype=jnp.int32)[:, None, None] == spike_slab, spike_depth, 1.0)
    extent_right = channel_extent(split_keys[6], sluggish_mask, sudden_spike)
    extent_left = channel_extent(split_keys[7], sluggish_mask, sudden_spike)
    angle_right = jax.random.uniform(split_keys[8], vector_shape, jnp.float32, -math.pi, math.pi)
    angle_left = jax.random.uniform(split_keys[9], vector_shape, jnp.float32, -math.pi, math.pi)
    real_added = jnp.where(on_diagonal, level_shift[..., :, None], 0.0)
    real_added = real_added + jnp.where(right_left, (extent_right * jnp.cos(angle_right))[..., :, None], 0.0)
    real_added = real_added + jnp.where(left_right, (extent_left * jnp.cos(angle_left))[..., None, :], 0.0)
    imag_added = jnp.where(on_diagonal, -broadening[..., :, None], 0.0)
    imag_added = imag_added + jnp.where(right_left, (extent_right * jnp.sin(angle_right))[..., :, None], 0.0)
    imag_added = imag_added + jnp.where(left_right, (extent_left * jnp.sin(angle_left))[..., None, :], 0.0)
    return (noise_part * noise_scale + jnp.stack([real_added, imag_added], axis=2)).astype(jnp.bfloat16)


def coupling_layout(key):
    layout_key = jax.random.fold_in(key, 71)
    split_keys = jax.random.split(layout_key, 3)
    off_row = jax.random.randint(split_keys[0], (SLAB_TOTAL, 1), 0, NBW)
    offset = jax.random.randint(split_keys[1], (SLAB_TOTAL, 1), 1, NBW)
    shuffle = jax.vmap(lambda subkey: jax.random.permutation(subkey, NNZ))(jax.random.split(split_keys[2], SLAB_TOTAL))
    return (off_row, offset, shuffle)


def draw_coupling_values(key, part):
    off_row, offset, shuffle = coupling_layout(key)
    key = jax.random.fold_in(key, 23)
    split_keys = jax.random.split(key, 2)
    array_shape = (SLAB_TOTAL, NNZ, BLK, BLK)
    noise_part = jnp.clip(jax.random.normal(split_keys[0], array_shape, jnp.float32), -6.0, 6.0)
    strength = jnp.exp(jax.random.uniform(split_keys[1], (SLAB_TOTAL, NNZ, BLK), jnp.float32, math.log(0.9), 0.0))
    off_factor = jnp.where(shuffle == NBW, 0.25, 1.0)
    strength = strength * off_factor[..., None]
    unit_mask = jnp.arange(BLK)[:, None] == jnp.arange(BLK)[None, :]
    return noise_part * (0.12 / math.sqrt(BLK)) + jnp.where(unit_mask, strength[..., :, None], 0.0)


def draw_coupling_index(key, part):
    off_row, offset, shuffle = coupling_layout(key)
    diagonal_rows = jnp.broadcast_to(jnp.arange(NBW, dtype=jnp.int32)[None, :], (SLAB_TOTAL, NBW))
    row_blocks = jnp.concatenate([diagonal_rows, off_row], axis=1)
    column_blocks = jnp.concatenate([diagonal_rows, (off_row + offset) % NBW], axis=1)
    row_blocks = jnp.take_along_axis(row_blocks, shuffle, axis=1)
    column_blocks = jnp.take_along_axis(column_blocks, shuffle, axis=1)
    return jnp.stack([row_blocks, column_blocks], axis=-1).astype(jnp.int32)


def draw_prev_lesser(key, part):
    key = jax.random.fold_in(key, 41)
    split_keys = jax.random.split(key, 2)
    array_shape = (SLAB_TOTAL, ENERGY_POINTS, 2, NBLK, BLK, BLK)
    noise_part = jnp.clip(jax.random.normal(split_keys[0], array_shape, jnp.float32), -6.0, 6.0)
    flipped = jnp.swapaxes(noise_part, 4, 5)
    real_part = 0.25 * (noise_part[:, :, 0] + flipped[:, :, 0])
    imag_part = 0.25 * (noise_part[:, :, 1] - flipped[:, :, 1])
    density = jnp.exp(jax.random.uniform(split_keys[1], (SLAB_TOTAL, ENERGY_POINTS, NBLK, BLK), jnp.float32, math.log(0.5), math.log(4.0)))
    unit_mask = jnp.arange(BLK)[:, None] == jnp.arange(BLK)[None, :]
    real_part = real_part + jnp.where(unit_mask, density[..., :, None], 0.0)
    return jnp.stack([real_part, imag_part], axis=2).reshape(SLAB_TOTAL, ENERGY_POINTS, 2, SLAB_ORBITALS, BLK)


def draw_phonon_shift(key, part):
    key = jax.random.fold_in(key, 53)
    split_keys = jax.random.split(key, 2)
    middle = jax.random.permutation(split_keys[0], jnp.arange(2, ENERGY_POINTS // 2, dtype=jnp.int32))[:NMODE - 2]
    shifts = jnp.concatenate([jnp.array([1], jnp.int32), middle, jnp.array([ENERGY_POINTS // 2], jnp.int32)])
    return jax.random.permutation(split_keys[1], shifts).astype(jnp.int32)


def setup_inputs(seed: int = 0) -> dict:
    key_of = jax.random.split(jax.random.key(seed), 7)
    green_ret = draw_green_ret(jax.random.fold_in(key_of[6], 71), 0)
    prev_lesser = draw_prev_lesser(jax.random.fold_in(key_of[6], 71), 0)
    coupling_index = draw_coupling_index(jax.random.fold_in(key_of[6], 71), 0)
    coupling_values = draw_coupling_values(jax.random.fold_in(key_of[6], 71), 0)
    phonon_shift = draw_phonon_shift(jax.random.fold_in(key_of[6], 71), 0)
    phonon_weight = jnp.clip(jnp.exp(jax.random.uniform(key_of[5], (2, NMODE), jnp.float32, math.log(0.1), math.log(0.5))), 0.1, 0.5)
    return dict(green_ret=green_ret, prev_lesser=prev_lesser, coupling_index=coupling_index, coupling_values=coupling_values, phonon_shift=phonon_shift, phonon_weight=phonon_weight)


FULL_PRECISION = lax.Precision.HIGHEST


def rounded(values):
    return lax.optimization_barrier(values.astype(jnp.bfloat16))


def product(pattern, left_factor, right_factor):
    return jnp.einsum(pattern, left_factor.astype(jnp.float32), right_factor.astype(jnp.float32), precision=FULL_PRECISION)


def complex_product(pattern, left_factor, right_factor):
    real_part = product(pattern, left_factor[0], right_factor[0]) - product(pattern, left_factor[1], right_factor[1])
    imag_part = product(pattern, left_factor[0], right_factor[1]) + product(pattern, left_factor[1], right_factor[0])
    return jnp.stack([real_part, imag_part])


def conjugate_product(pattern, left_factor, right_factor):
    real_part = product(pattern, left_factor[0], right_factor[0]) + product(pattern, left_factor[1], right_factor[1])
    imag_part = product(pattern, left_factor[1], right_factor[0]) - product(pattern, left_factor[0], right_factor[1])
    return jnp.stack([real_part, imag_part])


def adjoint(matrix):
    return jnp.stack([matrix[0].T, -matrix[1].T])


def block_adjoint(blocks):
    shaped = jnp.swapaxes(blocks.reshape(2, NBLK, BLK, BLK), 2, 3)
    return jnp.stack([shaped[0], -shaped[1]]).reshape(2, SLAB_ORBITALS, BLK)


def blocks_product(left_factor, right_factor):
    inner_size = left_factor.shape[-1]
    return complex_product("nak,knb->nab", left_factor.reshape(2, NBLK, BLK, inner_size), right_factor.reshape(2, inner_size, NBLK, BLK)).reshape(2, SLAB_ORBITALS, BLK)


def blocks_adjoint_product(left_factor, right_factor):
    inner_size = left_factor.shape[-1]
    return conjugate_product("nak,nbk->nab", left_factor.reshape(2, NBLK, BLK, inner_size), right_factor.reshape(2, NBLK, BLK, inner_size)).reshape(2, SLAB_ORBITALS, BLK)


def diagonal_blocks(green_fn):
    shaped = green_fn.astype(jnp.float32).reshape(2, NBLK, BLK, NBLK, BLK)
    return jnp.einsum("pnanb->pnab", shaped).reshape(2, SLAB_ORBITALS, BLK)


def dense_coupling(block_index, block_values):
    positions = jnp.arange(NBW, dtype=jnp.int32)[None, :]
    row_select = (block_index[:, 0:1] == positions).astype(jnp.float32)
    column_select = (block_index[:, 1:2] == positions).astype(jnp.float32)
    dense = jnp.einsum("br,bc,bij->ricj", row_select, column_select, block_values, precision=FULL_PRECISION)
    return dense.reshape(BW, BW)


def partner_weights(targets, sources, phonon_shift, phonon_weight):
    target_column = jnp.asarray(targets)[..., None]
    source_column = jnp.asarray(sources)[..., None]
    emission = jnp.where(source_column == target_column + phonon_shift, phonon_weight[0], 0.0)
    absorption = jnp.where(source_column == target_column - phonon_shift, phonon_weight[1], 0.0)
    return jnp.sum(emission + absorption, axis=-1)


def sandwich_left(coupling, matrix):
    return jnp.einsum("ki,pkl,lj->pij", coupling, matrix, coupling, precision=FULL_PRECISION)


def sandwich_right(coupling, matrix):
    return jnp.einsum("ik,pkl,jl->pij", coupling, matrix, coupling, precision=FULL_PRECISION)


def local_terms(green_fn, self_energy):
    sigma_rounded = rounded(self_energy).reshape(2, NBLK, BLK, BLK)
    scaled = rounded(complex_product("ank,nkl->anl", green_fn.reshape(2, SLAB_ORBITALS, NBLK, BLK), sigma_rounded).reshape(2, SLAB_ORBITALS, SLAB_ORBITALS))
    outer_right = conjugate_product("ik,jk->ij", scaled[:, SLAB_ORBITALS - BW:], green_fn)
    outer_left = conjugate_product("ik,jk->ij", scaled[:, :BW], green_fn[:, :BW])
    outer_blocks = blocks_adjoint_product(scaled, green_fn)
    return outer_right, outer_left, outer_blocks


def reference(green_ret, prev_lesser, coupling_index, coupling_values, phonon_shift, phonon_weight):
    energies = jnp.arange(ENERGY_POINTS, dtype=jnp.int32)
    weight_table = partner_weights(energies[:, None], energies[None, :], phonon_shift, phonon_weight)
    self_energy = jnp.einsum("ef,sfpak->sepak", weight_table, prev_lesser, precision=FULL_PRECISION)
    couplings = jax.vmap(dense_coupling)(coupling_index, coupling_values)

    def one_energy(energy):
        green_all = lax.dynamic_index_in_dim(green_ret, energy, 1, keepdims=False)
        sigma_slabs = lax.dynamic_index_in_dim(self_energy, energy, 1, keepdims=False)
        boundary_state = jnp.zeros((2, BW, BW), jnp.float32)
        forward_kept = []
        for slab_index in range(SLAB_TOTAL):
            green_fn = green_all[slab_index]
            outer_right, outer_left, outer_blocks = local_terms(green_fn, sigma_slabs[slab_index])
            corner = green_fn[:, SLAB_ORBITALS - BW:, :BW]
            right_block = conjugate_product("ik,jk->ij", complex_product("ik,kj->ij", corner, boundary_state), corner) + outer_right[:, :, SLAB_ORBITALS - BW:]
            coupled = rounded(complex_product("ik,kj->ij", green_fn[:, :, :BW], rounded(boundary_state)))
            far_right = outer_right + conjugate_product("ik,jk->ij", coupled[:, SLAB_ORBITALS - BW:], green_fn[:, :, :BW])
            left_block = outer_left + conjugate_product("ik,jk->ij", coupled[:, :BW], green_fn[:, :BW, :BW])
            lesser_local = outer_blocks + blocks_adjoint_product(coupled, green_fn[:, :, :BW])
            forward_kept.append((far_right, left_block, lesser_local))
            boundary_state = sandwich_left(couplings[slab_index], right_block)
        retarded_next = jnp.zeros((2, BW, BW), jnp.float32)
        lesser_next = jnp.zeros((2, BW, BW), jnp.float32)
        retarded_list = []
        lesser_list = []
        for slab_index in reversed(range(SLAB_TOTAL)):
            green_fn = green_all[slab_index]
            coupling = couplings[slab_index]
            far_right, left_block, lesser_local = forward_kept[slab_index]
            retarded_far = sandwich_right(coupling, retarded_next)
            lesser_far = sandwich_right(coupling, lesser_next)
            upper_corner = green_fn[:, :BW, SLAB_ORBITALS - BW:]
            corner = green_fn[:, SLAB_ORBITALS - BW:, :BW]
            through = complex_product("ik,kj->ij", upper_corner, retarded_far)
            mixed_term = complex_product("ik,kj->ij", through, far_right[:, :, :BW])
            retarded_next = green_fn[:, :BW, :BW].astype(jnp.float32) + complex_product("ik,kj->ij", through, corner)
            lesser_next = left_block + mixed_term + adjoint(mixed_term) + conjugate_product("ik,jk->ij", complex_product("ik,kj->ij", upper_corner, lesser_far), upper_corner)
            right_columns = green_fn[:, :, SLAB_ORBITALS - BW:]
            retarded_weighted = rounded(complex_product("ik,kj->ij", right_columns, rounded(retarded_far)))
            lesser_weighted = rounded(complex_product("ik,kj->ij", right_columns, rounded(lesser_far)))
            retarded = diagonal_blocks(green_fn) + blocks_product(retarded_weighted, green_fn[:, SLAB_ORBITALS - BW:, :])
            mixed_blocks = blocks_product(retarded_weighted, rounded(far_right))
            lesser = lesser_local + mixed_blocks + block_adjoint(mixed_blocks) + blocks_adjoint_product(lesser_weighted, right_columns)
            retarded_list.append(retarded)
            lesser_list.append(lesser)
        return jnp.stack(retarded_list[::-1]), jnp.stack(lesser_list[::-1])

    retarded_all, lesser_all = lax.map(one_energy, energies)
    return jnp.swapaxes(retarded_all, 0, 1), jnp.swapaxes(lesser_all, 0, 1)
```

```python
import functools

import jax
import jax.numpy as jnp
from jax import lax
from jax.experimental import pallas as pl
from jax.experimental.pallas import tpu as pltpu
from jax.sharding import PartitionSpec as P

SLAB_ORBITALS = 1536
BW = 256
BLK = 128
NBLK = 12
NBW = 2
PAIRS = SLAB_ORBITALS // BW
HALF = 4

FULL_PRECISION = lax.Precision.HIGHEST
MESH = pl.DeviceIdType.MESH
VMEM_LIMIT = 58 * 1024 * 1024
NN = (((1,), (0,)), ((), ()))
NT = (((1,), (1,)), ((), ()))

f32 = jnp.float32
bf16 = jnp.bfloat16


def dot(left, right, dims=NN):
    return lax.dot_general(left, right, dims, preferred_element_type=f32)


def split(value):
    high = value.astype(bf16)
    return high, (value - high.astype(f32)).astype(bf16)


def turned(value):
    width = value.shape[1] // 2
    return jnp.concatenate([-value[:, width:], value[:, :width]], axis=1)


def doubled(value):
    return jnp.concatenate([value, turned(value)], axis=0)


def product(left, right, dims=NN):
    left_high, left_low = split(left)
    right_high, right_low = split(right)
    main = doubled(right_high)
    return (
        dot(left_high, main, dims) + dot(left_low, main, dims) + dot(left_high, doubled(right_low), dims)
    )


def exact_left(left, right, dims=NN):
    right_high, right_low = split(right)
    return dot(left, doubled(right_high), dims) + dot(left, doubled(right_low), dims)


def exact_right(left, right, dims=NN):
    left_high, left_low = split(left)
    main = doubled(right)
    return dot(left_high, main, dims) + dot(left_low, main, dims)


def real_left(matrix, value):
    matrix_high, matrix_low = split(matrix)
    value_high, value_low = split(value)
    return dot(matrix_high, value_high) + dot(matrix_high, value_low) + dot(matrix_low, value_high)


def real_right(value, matrix):
    matrix_high, matrix_low = split(matrix)
    parts = []
    for part in (value[:, :BW], value[:, BW:]):
        high, low = split(part)
        parts.append(dot(high, matrix_high) + dot(low, matrix_high) + dot(high, matrix_low))
    return jnp.concatenate(parts, axis=1)


def beside(ref):
    return jnp.concatenate([ref[0], ref[1]], axis=1)


def adjoint(value):
    return jnp.concatenate([value[:, :BW].T, -value[:, BW:].T], axis=1)


class Place:
    def __init__(self):
        slab = lax.axis_index("slab")
        self.half = slab // HALF
        self.z = slab % HALF
        base = self.half * HALF
        self.right = base + (self.z + 1) % HALF
        self.left = base + (self.z + HALF - 1) % HALF
        self.across = (slab + HALF) % (2 * HALF)


def enter(place):
    barrier = pltpu.get_barrier_semaphore()
    for other in (place.left, place.right, place.across):
        pl.semaphore_signal(barrier, inc=1, device_id={"slab": other}, device_id_type=MESH)
    pl.semaphore_wait(barrier, 3)


class Gather:
    def __init__(self, place, slots, send, recv):
        z = place.z
        low, high = pl.ds(0, BW // 2), pl.ds(BW // 2, BW // 2)
        before, after, opposite = (z + 3) % HALF, (z + 1) % HALF, (z + 2) % HALF

        def copy(index, slot, rows, target):
            part = slots.at[slot, rows]
            return pltpu.make_async_remote_copy(
                src_ref=part,
                dst_ref=part,
                send_sem=send.at[index],
                recv_sem=recv.at[index],
                device_id={"slab": target},
                device_id_type=MESH,
            )

        self.first = [
            copy(0, z, low, place.right),
            copy(1, z, high, place.left),
            copy(2, z, high, place.right),
            copy(3, z, low, place.left),
        ]
        self.arrive = [
            copy(0, before, low, place.right),
            copy(1, after, high, place.left),
            copy(2, before, high, place.right),
            copy(3, after, low, place.left),
        ]
        self.relay = [copy(4, before, low, place.right), copy(5, after, high, place.left)]
        self.last = [copy(4, opposite, low, place.right), copy(5, opposite, high, place.left)]

    def start(self):
        for item in self.first:
            item.start()

    def forward(self):
        for index in (0, 1):
            self.arrive[index].wait_recv()
            self.relay[index].start()

    def finish(self):
        for item in self.arrive[2:] + self.last:
            item.wait_recv()
        for item in self.first + self.relay:
            item.wait_send()


def crossing(place, source, target, send, recv):
    return pltpu.make_async_remote_copy(
        src_ref=source,
        dst_ref=target,
        send_sem=send,
        recv_sem=recv,
        device_id={"slab": place.across},
        device_id_type=MESH,
    )


def early_kernel(
    g_rl, g_lr, g_ll, coupling, coupling_t,
    transfer, inward, through, far,
    corner, run, own, incoming, send, recv, cross_send, cross_recv,
):
    place = Place()
    z, half = place.z, place.half
    enter(place)
    turn = [Gather(place, ref, send.at[i], recv.at[i]) for i, ref in enumerate((transfer, inward, corner))]
    c_high, c_low = split(coupling[...])
    t_high, t_low = split(coupling_t[...])
    value = beside(g_rl)
    transfer[z] = dot(t_high, value) + dot(t_low, value)
    turn[0].start()
    parts = [dot(g_lr[i], c_high) + dot(g_lr[i], c_low) for i in (0, 1)]
    inward[z] = jnp.concatenate(parts, axis=1)
    turn[1].start()
    corner[z] = beside(g_ll).astype(f32)
    turn[2].start()
    for item in turn:
        item.forward()
    for item in turn:
        item.finish()

    own[...] = jnp.zeros_like(own)

    def step(index, _):
        j = HALF - 1 - index

        @pl.when(j == z)
        def _():
            own[...] = run[...]

        run[...] = corner[j] + product(product(inward[j], run[...]), transfer[j])
        return 0

    cross = crossing(place, run, incoming, cross_send, cross_recv)

    @pl.when(half == 1)
    def _():
        run[...] = corner[HALF - 1]

    @pl.when(half == 0)
    def _():
        cross.wait_recv()
        run[...] = incoming[...]

    lax.fori_loop(half, jnp.where(half == 1, HALF, HALF - 1 - z), step, 0)

    @pl.when(half == 1)
    def _():
        cross.start()
        cross.wait_send()

    @pl.when(half == 0)
    def _():
        own[...] = run[...]

    value = own[...]
    outer = real_right(value, coupling_t[...])
    through[...] = product(inward[z], outer)
    far[...] = real_left(coupling[...], outer).astype(bf16)


def sweep_kernel(
    transfer, inward, through, coupling, coupling_t, g_ll, g_rl, outer_rr, outer_rl, outer_ll,
    state, far,
    source, driven, run, own, incoming, send, recv, cross_send, cross_recv,
):
    place = Place()
    z, half = place.z, place.half
    enter(place)
    turn = Gather(place, source, send.at[0], recv.at[0])
    source[z] = real_left(coupling_t[...], real_right(beside(outer_rr), coupling[...]))
    turn.start()
    turn.forward()
    turn.finish()

    own[...] = jnp.zeros_like(own)

    def forward_step(j, _):
        @pl.when(j == z)
        def _():
            own[...] = run[...]

        factor = transfer[j]
        run[...] = product(product(factor, run[...]), factor, NT) + source[j]
        return 0

    up = crossing(place, run, incoming, cross_send.at[0], cross_recv.at[0])

    @pl.when(half == 0)
    def _():
        run[...] = source[0]

    @pl.when(half == 1)
    def _():
        up.wait_recv()
        run[...] = incoming[...]

    lax.fori_loop(1 - half, jnp.where(half == 0, HALF, z), forward_step, 0)

    @pl.when(half == 0)
    def _():
        up.start()

    @pl.when(half == 1)
    def _():
        own[...] = run[...]

    value = own[...]
    state[...] = value.astype(bf16)
    left = beside(g_ll)
    tail = exact_right(value, left, NT)
    right = exact_left(jnp.concatenate([left, beside(g_rl)], axis=0), tail)
    mixed = product(through[...], beside(outer_rl) + right[BW:])
    turn = Gather(place, driven, send.at[1], recv.at[1])
    driven[z] = beside(outer_ll) + right[:BW] + mixed + adjoint(mixed)
    turn.start()
    turn.forward()
    turn.finish()

    @pl.when(half == 0)
    def _():
        up.wait_send()

    own[...] = jnp.zeros_like(own)

    def backward_step(index, _):
        j = HALF - 1 - index

        @pl.when(j == z)
        def _():
            own[...] = run[...]

        factor = inward[j]
        run[...] = product(product(factor, run[...]), factor, NT) + driven[j]
        return 0

    down = crossing(place, run, incoming, cross_send.at[1], cross_recv.at[1])

    @pl.when(half == 1)
    def _():
        run[...] = driven[HALF - 1]

    @pl.when(half == 0)
    def _():
        down.wait_recv()
        run[...] = incoming[...]

    lax.fori_loop(half, jnp.where(half == 1, HALF, HALF - 1 - z), backward_step, 0)

    @pl.when(half == 1)
    def _():
        down.start()

    @pl.when(half == 0)
    def _():
        own[...] = run[...]

    far[...] = real_left(coupling[...], real_right(own[...], coupling_t[...])).astype(bf16)

    @pl.when(half == 1)
    def _():
        down.wait_send()


def local_kernel(green, sigma, outer_right, outer_left, outer_blocks, scaled):
    rows = 512

    def scale(n, _):
        columns = pl.ds(pl.multiple_of(n * BLK, BLK), BLK)
        real, imag = sigma[0, columns, :], sigma[1, columns, :]
        factor = jnp.concatenate(
            [jnp.concatenate([real, imag], axis=1), jnp.concatenate([-imag, real], axis=1)], axis=0
        )
        for start in range(0, SLAB_ORBITALS, rows):
            span = pl.ds(start, rows)
            piece = jnp.concatenate([green[0, span, columns], green[1, span, columns]], axis=1)
            result = dot(piece, factor).astype(bf16)
            scaled[0, span, columns] = result[:, :BLK]
            scaled[1, span, columns] = result[:, BLK:]
            scaled[2, span, columns] = -result[:, :BLK]
        return 0

    lax.fori_loop(0, NBLK, scale, 0)
    last = pl.ds(SLAB_ORBITALS - BW, BW)

    def against(left_rows, right_rows):
        first = scaled[0:2, left_rows, :].reshape(2 * BW, SLAB_ORBITALS)
        second = scaled[1:3, left_rows, :].reshape(2 * BW, SLAB_ORBITALS)
        total = dot(first, green[0, right_rows, :], NT) + dot(second, green[1, right_rows, :], NT)
        return total.reshape(2, BW, BW)

    def pair(m, _):
        span = pl.ds(pl.multiple_of(m * BW, BW), BW)
        outer_right[m] = against(last, span)
        local = against(span, span)
        first = pl.ds(pl.multiple_of(m * BW, BW), BLK)
        second = pl.ds(pl.multiple_of(m * BW + BLK, BLK), BLK)
        outer_blocks[:, first, :] = local[:, :BLK, :BLK]
        outer_blocks[:, second, :] = local[:, BLK:, BLK:]

        @pl.when(m == 0)
        def _():
            outer_left[...] = local

        return 0

    lax.fori_loop(0, PAIRS, pair, 0)


def final_kernel(
    green, state, retarded_far, lesser_far, outer_right, outer_blocks,
    retarded_out, lesser_out,
    coupled, lesser_weighted, retarded_weighted,
):
    rows = 512
    left = pl.ds(0, BW)
    last = pl.ds(SLAB_ORBITALS - BW, BW)
    state_factor = doubled(state[...])
    retarded_factor = doubled(retarded_far[...])
    lesser_factor = doubled(lesser_far[...])
    for start in range(0, SLAB_ORBITALS, rows):
        span = pl.ds(start, rows)
        piece = jnp.concatenate([green[0, span, left], green[1, span, left]], axis=1)
        result = dot(piece, state_factor).astype(bf16)
        coupled[0, span, :] = result[:, :BW]
        coupled[1, span, :] = result[:, BW:]
        coupled[2, span, :] = -result[:, :BW]
        piece = jnp.concatenate([green[0, span, last], green[1, span, last]], axis=1)
        retarded_weighted[span, :] = dot(piece, retarded_factor).astype(bf16)
        result = dot(piece, lesser_factor).astype(bf16)
        lesser_weighted[0, span, :] = result[:, :BW]
        lesser_weighted[1, span, :] = result[:, BW:]
        lesser_weighted[2, span, :] = -result[:, :BW]

    def against(values, left_rows, right_rows, columns):
        first = values[0:2, left_rows, :].reshape(2 * BW, BW)
        second = values[1:3, left_rows, :].reshape(2 * BW, BW)
        total = dot(first, green[0, right_rows, columns], NT) + dot(second, green[1, right_rows, columns], NT)
        return total.reshape(2, BW, BW)

    def pair(m, _):
        span = pl.ds(pl.multiple_of(m * BW, BW), BW)
        far_right = (outer_right[m] + against(coupled, last, span, left)).astype(bf16)
        weighted = retarded_weighted[span, :]
        retarded = dot(weighted, doubled(jnp.concatenate([green[0, last, span], green[1, last, span]], axis=1)))
        mixed = dot(weighted, doubled(jnp.concatenate([far_right[0], far_right[1]], axis=1)))
        lesser = against(coupled, span, span, left) + against(lesser_weighted, span, span, last)
        for k in (0, 1):
            start = pl.multiple_of(m * BW + k * BLK, BLK)
            block = pl.ds(start, BLK)
            here = slice(k * BLK, (k + 1) * BLK)
            for part in (0, 1):
                there = slice(part * BW + k * BLK, part * BW + (k + 1) * BLK)
                retarded_out[part, block, :] = green[part, block, block].astype(f32) + retarded[here, there]
                mix = mixed[here, there]
                mirrored = mix.T if part == 0 else -mix.T
                lesser_out[part, block, :] = outer_blocks[part, block, :] + lesser[part, here, here] + mix + mirrored
        return 0

    lax.fori_loop(0, PAIRS, pair, 0)


def whole(count):
    return [pl.BlockSpec(memory_space=pltpu.VMEM)] * count


def shape(dims, dtype=f32):
    return jax.ShapeDtypeStruct(dims, dtype)


WIDE = (BW, 2 * BW)


def early(g_rl, g_lr, g_ll, coupling, coupling_t):
    return pl.pallas_call(
        early_kernel,
        out_shape=[shape((HALF,) + WIDE), shape((HALF,) + WIDE), shape(WIDE), shape(WIDE, bf16)],
        in_specs=whole(5),
        out_specs=whole(4),
        scratch_shapes=[
            pltpu.VMEM((HALF,) + WIDE, f32),
            pltpu.VMEM(WIDE, f32),
            pltpu.VMEM(WIDE, f32),
            pltpu.VMEM(WIDE, f32),
            pltpu.SemaphoreType.DMA((3, 6)),
            pltpu.SemaphoreType.DMA((3, 6)),
            pltpu.SemaphoreType.DMA,
            pltpu.SemaphoreType.DMA,
        ],
        compiler_params=pltpu.CompilerParams(
            collective_id=0, has_side_effects=True, vmem_limit_bytes=VMEM_LIMIT
        ),
    )(g_rl, g_lr, g_ll, coupling, coupling_t)


def sweep(*operands):
    return pl.pallas_call(
        sweep_kernel,
        out_shape=[shape(WIDE, bf16), shape(WIDE, bf16)],
        in_specs=whole(len(operands)),
        out_specs=whole(2),
        scratch_shapes=[
            pltpu.VMEM((HALF,) + WIDE, f32),
            pltpu.VMEM((HALF,) + WIDE, f32),
            pltpu.VMEM(WIDE, f32),
            pltpu.VMEM(WIDE, f32),
            pltpu.VMEM(WIDE, f32),
            pltpu.SemaphoreType.DMA((2, 6)),
            pltpu.SemaphoreType.DMA((2, 6)),
            pltpu.SemaphoreType.DMA((2,)),
            pltpu.SemaphoreType.DMA((2,)),
        ],
        compiler_params=pltpu.CompilerParams(
            collective_id=1, has_side_effects=True, vmem_limit_bytes=VMEM_LIMIT
        ),
    )(*operands)


def local_terms(green, sigma):
    return pl.pallas_call(
        local_kernel,
        out_shape=[
            shape((PAIRS, 2, BW, BW)),
            shape((2, BW, BW)),
            shape((2, SLAB_ORBITALS, BLK)),
        ],
        in_specs=whole(2),
        out_specs=whole(3),
        scratch_shapes=[pltpu.VMEM((3, SLAB_ORBITALS, SLAB_ORBITALS), bf16)],
        compiler_params=pltpu.CompilerParams(vmem_limit_bytes=VMEM_LIMIT),
    )(green, sigma)


def final_terms(*operands):
    return pl.pallas_call(
        final_kernel,
        out_shape=[shape((2, SLAB_ORBITALS, BLK)), shape((2, SLAB_ORBITALS, BLK))],
        in_specs=whole(len(operands)),
        out_specs=whole(2),
        scratch_shapes=[
            pltpu.VMEM((3, SLAB_ORBITALS, BW), bf16),
            pltpu.VMEM((3, SLAB_ORBITALS, BW), bf16),
            pltpu.VMEM((SLAB_ORBITALS, 2 * BW), bf16),
        ],
        compiler_params=pltpu.CompilerParams(vmem_limit_bytes=VMEM_LIMIT),
    )(*operands)


def dense_coupling(block_index, block_values):
    positions = jnp.arange(NBW, dtype=jnp.int32)[None, :]
    row_select = (block_index[:, 0:1] == positions).astype(jnp.float32)
    column_select = (block_index[:, 1:2] == positions).astype(jnp.float32)
    dense = jnp.einsum(
        "br,bc,bij->ricj", row_select, column_select, block_values, precision=FULL_PRECISION
    )
    return dense.reshape(BW, BW)


def partner_weights(targets, sources, phonon_shift, phonon_weight):
    target_column = jnp.asarray(targets)[..., None]
    source_column = jnp.asarray(sources)[..., None]
    emission = jnp.where(source_column == target_column + phonon_shift, phonon_weight[0], 0.0)
    absorption = jnp.where(source_column == target_column - phonon_shift, phonon_weight[1], 0.0)
    return jnp.sum(emission + absorption, axis=-1)


def slab_work(green, sigma, coupling):
    lead, tail = slice(0, BW), slice(SLAB_ORBITALS - BW, SLAB_ORBITALS)
    g_ll, g_rl, g_lr = green[:, lead, lead], green[:, tail, lead], green[:, lead, tail]
    coupling_t = coupling.T
    transfer, inward, through, retarded_far = early(g_rl, g_lr, g_ll, coupling, coupling_t)
    outer_right, outer_left, outer_blocks = local_terms(green, sigma)
    state, lesser_far = sweep(
        transfer, inward, through, coupling, coupling_t, g_ll, g_rl,
        outer_right[PAIRS - 1], outer_right[0], outer_left,
    )
    return final_terms(green, state, retarded_far, lesser_far, outer_right, outer_blocks)


def body(green_ret, prev_lesser, coupling_index, coupling_values, phonon_shift, phonon_weight):
    green = green_ret[0, 0]
    coupling = dense_coupling(coupling_index[0], coupling_values[0])
    my_energy = lax.axis_index("energy")
    received = lax.all_gather(prev_lesser[0, 0], "energy", axis=0, tiled=False)
    sources = jnp.arange(received.shape[0], dtype=jnp.int32)
    weights = partner_weights(my_energy, sources, phonon_shift, phonon_weight)
    sigma = sum(weights[f] * received[f] for f in range(received.shape[0])).astype(bf16)
    retarded, lesser = slab_work(green, sigma, coupling)
    return retarded[None, None], lesser[None, None]


def solution(mesh):
    placed = (
        P("slab", "energy", None, None, None),
        P("slab", "energy", None, None, None),
        P("slab", None, None),
        P("slab", None, None, None),
        P(),
        P(),
    )
    return jax.shard_map(
        body,
        mesh=mesh,
        in_specs=placed,
        out_specs=(P("slab", "energy", None, None, None), P("slab", "energy", None, None, None)),
        check_vma=False,
    )
```

```python
import functools

import jax
import jax.numpy as jnp
from jax import lax
from jax.experimental import pallas as pl
from jax.experimental.pallas import tpu as pltpu
from jax.sharding import PartitionSpec as P

SLAB_ORBITALS = 1536
BW = 256
BLK = 128
NBLK = 12
NBW = 2
PAIRS = SLAB_ORBITALS // BW
HALF = 4

FULL_PRECISION = lax.Precision.HIGHEST
MESH = pl.DeviceIdType.MESH
VMEM_LIMIT = 58 * 1024 * 1024
NN = (((1,), (0,)), ((), ()))
NT = (((1,), (1,)), ((), ()))

f32 = jnp.float32
bf16 = jnp.bfloat16


def dot(left, right, dims=NN):
    return lax.dot_general(left, right, dims, preferred_element_type=f32)


def split(value):
    high = value.astype(bf16)
    return high, (value - high.astype(f32)).astype(bf16)


def turned(value):
    width = value.shape[1] // 2
    return jnp.concatenate([-value[:, width:], value[:, :width]], axis=1)


def doubled(value):
    return jnp.concatenate([value, turned(value)], axis=0)


def product(left, right, dims=NN):
    left_high, left_low = split(left)
    right_high, right_low = split(right)
    main = doubled(right_high)
    return (
        dot(left_high, main, dims) + dot(left_low, main, dims) + dot(left_high, doubled(right_low), dims)
    )


def real_left(matrix, value):
    matrix_high, matrix_low = split(matrix)
    value_high, value_low = split(value)
    return dot(matrix_high, value_high) + dot(matrix_high, value_low) + dot(matrix_low, value_high)


def real_right(value, matrix):
    matrix_high, matrix_low = split(matrix)
    parts = []
    for part in (value[:, :BW], value[:, BW:]):
        high, low = split(part)
        parts.append(dot(high, matrix_high) + dot(low, matrix_high) + dot(high, matrix_low))
    return jnp.concatenate(parts, axis=1)


def beside(ref):
    return jnp.concatenate([ref[0], ref[1]], axis=1)


def adjoint(value):
    return jnp.concatenate([value[:, :BW].T, -value[:, BW:].T], axis=1)


class Place:
    def __init__(self):
        slab, energy = lax.axis_index("slab"), lax.axis_index("energy")
        self.half = slab // HALF
        self.z = slab % HALF
        base = self.half * HALF
        self.right = {"slab": base + (self.z + 1) % HALF}
        self.left = {"slab": base + (self.z + HALF - 1) % HALF}
        other_half = (slab + HALF) % (2 * HALF)
        flipped = energy + 2 - 4 * (energy // 2 % 2)
        self.across = {"slab": other_half}
        self.across_flipped = {"slab": other_half, "energy": flipped}
        self.core = {"energy": energy + 1 - 2 * (energy % 2)}
        self.x_next = {"energy": (energy + 4) % 16}
        self.x_before = {"energy": (energy + 12) % 16}


def enter(others):
    barrier = pltpu.get_barrier_semaphore()
    for other in others:
        pl.semaphore_signal(barrier, inc=1, device_id=other, device_id_type=MESH)
    pl.semaphore_wait(barrier, len(others))


def sending(source, target, send, recv, device):
    return pltpu.make_async_remote_copy(
        src_ref=source, dst_ref=target, send_sem=send, recv_sem=recv, device_id=device, device_id_type=MESH
    )


class Gather:
    def __init__(self, place, slots, send, recv):
        z = place.z
        low, high = pl.ds(0, BW // 2), pl.ds(BW // 2, BW // 2)
        before, after, opposite = (z + 3) % HALF, (z + 1) % HALF, (z + 2) % HALF

        def copy(index, slot, rows, target):
            part = slots.at[slot, rows]
            return sending(part, part, send.at[index], recv.at[index], target)

        self.first = [
            copy(0, z, low, place.right),
            copy(1, z, high, place.left),
            copy(2, z, high, place.right),
            copy(3, z, low, place.left),
        ]
        self.arrive = [
            copy(0, before, low, place.right),
            copy(1, after, high, place.left),
            copy(2, before, high, place.right),
            copy(3, after, low, place.left),
        ]
        self.relay = [copy(4, before, low, place.right), copy(5, after, high, place.left)]
        self.last = [copy(4, opposite, low, place.right), copy(5, opposite, high, place.left)]

    def start(self):
        for item in self.first:
            item.start()

    def forward(self):
        for index in (0, 1):
            self.arrive[index].wait_recv()
            self.relay[index].start()

    def finish(self):
        for item in self.arrive[2:] + self.last:
            item.wait_recv()
        for item in self.first + self.relay:
            item.wait_send()


CHUNKS = 4
STACKED = 2 * SLAB_ORBITALS
CHUNK = STACKED // CHUNKS
PART = CHUNK // 2


def phonon_kernel(
    weights, previous, g_rl, g_lr, g_ll, coupling, coupling_t,
    sigma, transfer, inward, corner,
    others, relay, two_away, after, before, passing, from_before, from_after, mine,
    z_send, z_recv, y_send, y_recv, core_send, core_recv, x_send, x_recv,
):
    place = Place()
    enter([place.left, place.right, place.across, place.across_flipped, place.core, place.x_next, place.x_before])
    z = place.z

    def low(c):
        return pl.ds(c * CHUNK, PART)

    def high(c):
        return pl.ds(c * CHUNK + PART, PART)

    def full(c):
        return pl.ds(c * CHUNK, CHUNK)

    steps = range(CHUNKS)

    def over_y(kind, source, target, device):
        return [sending(source(c), target(c), y_send.at[kind, c], y_recv.at[kind, c], device) for c in steps]

    def over_core(kind, source, target):
        return [sending(source(c), target(c), core_send.at[kind, c], core_recv.at[kind, c], place.core) for c in steps]

    def over_x(kind, source, target, device):
        return [sending(source(c), target(c), x_send.at[kind, c], x_recv.at[kind, c], device) for c in steps]

    hop_a = over_y(0, lambda c: previous.at[low(c)], lambda c: relay.at[0, c], place.across)
    end_a = over_y(1, lambda c: relay.at[0, c], lambda c: others.at[1, low(c)], place.across_flipped)
    hop_b = over_y(2, lambda c: previous.at[high(c)], lambda c: relay.at[1, c], place.across_flipped)
    end_b = over_y(3, lambda c: relay.at[1, c], lambda c: others.at[1, high(c)], place.across)
    core_own = over_core(0, lambda c: previous.at[full(c)], lambda c: others.at[0, full(c)])
    core_more = over_core(1, lambda c: others.at[1, full(c)], lambda c: others.at[2, full(c)])
    two_low = over_x(0, lambda c: two_away.at[low(c)], lambda c: passing.at[0, c], place.x_next)
    two_high = over_x(1, lambda c: two_away.at[high(c)], lambda c: passing.at[1, c], place.x_before)
    after_high = over_x(2, lambda c: after.at[high(c)], lambda c: from_before.at[high(c)], place.x_next)
    before_low = over_x(3, lambda c: before.at[low(c)], lambda c: from_after.at[low(c)], place.x_before)
    after_low = over_x(4, lambda c: after.at[low(c)], lambda c: from_before.at[low(c)], place.x_next)
    before_high = over_x(5, lambda c: before.at[high(c)], lambda c: from_after.at[high(c)], place.x_before)

    for c in (0, 1):
        hop_a[c].start()
        hop_b[c].start()
    for c in steps:
        core_own[c].start()

    turn = [Gather(place, ref, z_send.at[i], z_recv.at[i]) for i, ref in enumerate((transfer, inward, corner))]
    c_high, c_low = split(coupling[...])
    t_high, t_low = split(coupling_t[...])
    value = beside(g_rl)
    transfer[z] = dot(t_high, value) + dot(t_low, value)
    turn[0].start()
    parts = [dot(g_lr[i], c_high) + dot(g_lr[i], c_low) for i in (0, 1)]
    inward[z] = jnp.concatenate(parts, axis=1)
    turn[1].start()
    corner[z] = beside(g_ll).astype(f32)
    turn[2].start()

    def pass_on(c):
        hop_a[c].wait_recv()
        end_a[c].start()
        hop_b[c].wait_recv()
        end_b[c].start()
        if c + 2 < CHUNKS:
            hop_a[c + 2].start()
            hop_b[c + 2].start()

    def weigh(c):
        end_a[c].wait_recv()
        end_b[c].wait_recv()
        core_more[c].start()
        core_own[c].wait_recv()
        core_more[c].wait_recv()
        rows = full(c)
        pieces = [previous[rows, :], others[0, rows, :], others[1, rows, :], others[2, rows, :]]

        def weighted(target):
            total = weights[4 * target] * pieces[0]
            for source in (1, 2, 3):
                total = total + weights[4 * target + source] * pieces[source]
            return total

        two_away[rows, :] = weighted(2)
        two_low[c].start()
        two_high[c].start()
        after[rows, :] = weighted(1)
        after_high[c].start()
        before[rows, :] = weighted(3)
        before_low[c].start()
        mine[rows, :] = weighted(0)

    def add_passing(c):
        two_low[c].wait_recv()
        after[low(c), :] = after[low(c), :] + passing[0, c]
        after_low[c].start()
        two_high[c].wait_recv()
        before[high(c), :] = before[high(c), :] + passing[1, c]
        before_high[c].start()

    def finish(c):
        for item in (after_high, before_low, after_low, before_high):
            item[c].wait_recv()
        rows = full(c)
        sigma[rows, :] = (mine[rows, :] + from_before[rows, :] + from_after[rows, :]).astype(bf16)

    for t in range(CHUNKS + 3):
        if t < CHUNKS:
            pass_on(t)
        if t < 3:
            turn[t].forward()
        if 0 <= t - 1 < CHUNKS:
            weigh(t - 1)
        if 0 <= t - 2 < CHUNKS:
            add_passing(t - 2)
        if 0 <= t - 3 < CHUNKS:
            finish(t - 3)
    for item in turn:
        item.finish()
    for group in (
        hop_a, end_a, hop_b, end_b, core_own, core_more,
        two_low, two_high, after_high, before_low, after_low, before_high,
    ):
        for item in group:
            item.wait_send()


def sweep_kernel(
    transfer, inward, corner, coupling, coupling_t, g_ll, g_rl, outer_rr, outer_rl, outer_ll,
    state, retarded_far, lesser_far,
    source, driven, run, own, kept, through, incoming, send, recv, cross_send, cross_recv,
):
    place = Place()
    z, half = place.z, place.half
    enter([place.left, place.right, place.across])

    def crossing(index, ref):
        return sending(ref, incoming.at[index], cross_send.at[index], cross_recv.at[index], place.across)

    over = crossing(0, kept)
    up = crossing(1, run)
    down = crossing(2, run)

    turn = Gather(place, source, send.at[0], recv.at[0])
    source[z] = real_left(coupling_t[...], real_right(beside(outer_rr), coupling[...]))
    turn.start()
    turn.forward()

    own[...] = jnp.zeros_like(own)

    def retarded_step(index, _):
        j = HALF - 1 - index

        @pl.when(j == z)
        def _():
            own[...] = kept[...]

        kept[...] = corner[j] + product(product(inward[j], kept[...]), transfer[j])
        return 0

    def use_retarded():
        outer = real_right(own[...], coupling_t[...])
        through[...] = product(inward[z], outer)
        retarded_far[...] = real_left(coupling[...], outer).astype(bf16)

    @pl.when(half == 1)
    def _():
        kept[...] = corner[HALF - 1]
        lax.fori_loop(1, HALF, retarded_step, 0)
        over.start()
        use_retarded()

    turn.finish()

    def forward_step(j, _):
        @pl.when(j == z)
        def _():
            own[...] = run[...]

        factor = transfer[j]
        run[...] = product(product(factor, run[...]), factor, NT) + source[j]
        return 0

    @pl.when(half == 0)
    def _():
        run[...] = source[0]
        lax.fori_loop(1, HALF, forward_step, 0)
        up.start()
        state[...] = own[...].astype(bf16)
        over.wait_recv()
        kept[...] = incoming[0]
        lax.fori_loop(0, HALF - 1 - z, retarded_step, 0)
        own[...] = kept[...]
        use_retarded()

    @pl.when(half == 1)
    def _():
        up.wait_recv()
        run[...] = incoming[1]
        lax.fori_loop(0, z, forward_step, 0)
        state[...] = run[...].astype(bf16)

    left = beside(g_ll)
    coupled = dot(jnp.concatenate([left, beside(g_rl)], axis=0), doubled(state[...])).astype(bf16)
    right = dot(coupled, doubled(left), NT)
    mixed = product(through[...], beside(outer_rl) + right[BW:])
    turn = Gather(place, driven, send.at[1], recv.at[1])
    driven[z] = beside(outer_ll) + right[:BW] + mixed + adjoint(mixed)
    turn.start()
    turn.forward()
    turn.finish()

    @pl.when(half == 0)
    def _():
        up.wait_send()

    own[...] = jnp.zeros_like(own)

    def backward_step(index, _):
        j = HALF - 1 - index

        @pl.when(j == z)
        def _():
            own[...] = run[...]

        factor = inward[j]
        run[...] = product(product(factor, run[...]), factor, NT) + driven[j]
        return 0

    @pl.when(half == 1)
    def _():
        run[...] = driven[HALF - 1]
        lax.fori_loop(1, HALF, backward_step, 0)
        down.start()

    @pl.when(half == 0)
    def _():
        down.wait_recv()
        run[...] = incoming[2]
        lax.fori_loop(0, HALF - 1 - z, backward_step, 0)
        own[...] = run[...]

    lesser_far[...] = real_left(coupling[...], real_right(own[...], coupling_t[...])).astype(bf16)

    @pl.when(half == 1)
    def _():
        over.wait_send()
        down.wait_send()


def local_kernel(green, sigma, outer_right, outer_left, outer_blocks, scaled):
    rows = 512

    def scale(n, _):
        columns = pl.ds(pl.multiple_of(n * BLK, BLK), BLK)
        real, imag = sigma[0, columns, :], sigma[1, columns, :]
        factor = jnp.concatenate(
            [jnp.concatenate([real, imag], axis=1), jnp.concatenate([-imag, real], axis=1)], axis=0
        )
        for start in range(0, SLAB_ORBITALS, rows):
            span = pl.ds(start, rows)
            piece = jnp.concatenate([green[0, span, columns], green[1, span, columns]], axis=1)
            result = dot(piece, factor).astype(bf16)
            scaled[0, span, columns] = result[:, :BLK]
            scaled[1, span, columns] = result[:, BLK:]
            scaled[2, span, columns] = -result[:, :BLK]
        return 0

    lax.fori_loop(0, NBLK, scale, 0)
    last = pl.ds(SLAB_ORBITALS - BW, BW)

    def against(left_rows, right_rows):
        first = scaled[0:2, left_rows, :].reshape(2 * BW, SLAB_ORBITALS)
        second = scaled[1:3, left_rows, :].reshape(2 * BW, SLAB_ORBITALS)
        total = dot(first, green[0, right_rows, :], NT) + dot(second, green[1, right_rows, :], NT)
        return total.reshape(2, BW, BW)

    def pair(m, _):
        span = pl.ds(pl.multiple_of(m * BW, BW), BW)
        outer_right[m] = against(last, span)
        local = against(span, span)
        first = pl.ds(pl.multiple_of(m * BW, BW), BLK)
        second = pl.ds(pl.multiple_of(m * BW + BLK, BLK), BLK)
        outer_blocks[:, first, :] = local[:, :BLK, :BLK]
        outer_blocks[:, second, :] = local[:, BLK:, BLK:]

        @pl.when(m == 0)
        def _():
            outer_left[...] = local

        return 0

    lax.fori_loop(0, PAIRS, pair, 0)


def final_kernel(
    green, state, retarded_far, lesser_far, outer_right, outer_blocks,
    retarded_out, lesser_out,
    coupled, lesser_weighted, retarded_weighted,
):
    rows = 512
    left = pl.ds(0, BW)
    last = pl.ds(SLAB_ORBITALS - BW, BW)
    state_factor = doubled(state[...])
    retarded_factor = doubled(retarded_far[...])
    lesser_factor = doubled(lesser_far[...])
    for start in range(0, SLAB_ORBITALS, rows):
        span = pl.ds(start, rows)
        piece = jnp.concatenate([green[0, span, left], green[1, span, left]], axis=1)
        result = dot(piece, state_factor).astype(bf16)
        coupled[0, span, :] = result[:, :BW]
        coupled[1, span, :] = result[:, BW:]
        coupled[2, span, :] = -result[:, :BW]
        piece = jnp.concatenate([green[0, span, last], green[1, span, last]], axis=1)
        retarded_weighted[span, :] = dot(piece, retarded_factor).astype(bf16)
        result = dot(piece, lesser_factor).astype(bf16)
        lesser_weighted[0, span, :] = result[:, :BW]
        lesser_weighted[1, span, :] = result[:, BW:]
        lesser_weighted[2, span, :] = -result[:, :BW]

    def against(values, left_rows, right_rows, columns):
        first = values[0:2, left_rows, :].reshape(2 * BW, BW)
        second = values[1:3, left_rows, :].reshape(2 * BW, BW)
        total = dot(first, green[0, right_rows, columns], NT) + dot(second, green[1, right_rows, columns], NT)
        return total.reshape(2, BW, BW)

    def pair(m, _):
        span = pl.ds(pl.multiple_of(m * BW, BW), BW)
        far_right = (outer_right[m] + against(coupled, last, span, left)).astype(bf16)
        weighted = retarded_weighted[span, :]
        retarded = dot(weighted, doubled(jnp.concatenate([green[0, last, span], green[1, last, span]], axis=1)))
        mixed = dot(weighted, doubled(jnp.concatenate([far_right[0], far_right[1]], axis=1)))
        lesser = against(coupled, span, span, left) + against(lesser_weighted, span, span, last)
        for k in (0, 1):
            start = pl.multiple_of(m * BW + k * BLK, BLK)
            block = pl.ds(start, BLK)
            here = slice(k * BLK, (k + 1) * BLK)
            for part in (0, 1):
                there = slice(part * BW + k * BLK, part * BW + (k + 1) * BLK)
                retarded_out[part, block, :] = green[part, block, block].astype(f32) + retarded[here, there]
                mix = mixed[here, there]
                mirrored = mix.T if part == 0 else -mix.T
                lesser_out[part, block, :] = outer_blocks[part, block, :] + lesser[part, here, here] + mix + mirrored
        return 0

    lax.fori_loop(0, PAIRS, pair, 0)


def whole(count):
    return [pl.BlockSpec(memory_space=pltpu.VMEM)] * count


def shape(dims, dtype=f32):
    return jax.ShapeDtypeStruct(dims, dtype)


WIDE = (BW, 2 * BW)


def phonon(weights, previous, *operands):
    stacked = pltpu.VMEM((STACKED, BLK), f32)
    dma = pltpu.SemaphoreType.DMA
    return pl.pallas_call(
        phonon_kernel,
        out_shape=[shape((STACKED, BLK), bf16)] + [shape((HALF,) + WIDE)] * 3,
        in_specs=[pl.BlockSpec(memory_space=pltpu.SMEM)] + whole(1 + len(operands)),
        out_specs=whole(4),
        scratch_shapes=[
            pltpu.VMEM((3, STACKED, BLK), f32),
            pltpu.VMEM((2, CHUNKS, PART, BLK), f32),
            stacked,
            stacked,
            stacked,
            pltpu.VMEM((2, CHUNKS, PART, BLK), f32),
            stacked,
            stacked,
            stacked,
            dma((3, 6)),
            dma((3, 6)),
            dma((4, CHUNKS)),
            dma((4, CHUNKS)),
            dma((2, CHUNKS)),
            dma((2, CHUNKS)),
            dma((6, CHUNKS)),
            dma((6, CHUNKS)),
        ],
        compiler_params=pltpu.CompilerParams(
            collective_id=0, has_side_effects=True, vmem_limit_bytes=VMEM_LIMIT
        ),
    )(weights, previous, *operands)


def sweep(*operands):
    wide = pltpu.VMEM(WIDE, f32)
    dma = pltpu.SemaphoreType.DMA
    return pl.pallas_call(
        sweep_kernel,
        out_shape=[shape(WIDE, bf16)] * 3,
        in_specs=whole(len(operands)),
        out_specs=whole(3),
        scratch_shapes=[
            pltpu.VMEM((HALF,) + WIDE, f32),
            pltpu.VMEM((HALF,) + WIDE, f32),
            wide,
            wide,
            wide,
            wide,
            pltpu.VMEM((3,) + WIDE, f32),
            dma((2, 6)),
            dma((2, 6)),
            dma((3,)),
            dma((3,)),
        ],
        compiler_params=pltpu.CompilerParams(
            collective_id=1, has_side_effects=True, vmem_limit_bytes=VMEM_LIMIT
        ),
    )(*operands)


def local_terms(green, sigma):
    return pl.pallas_call(
        local_kernel,
        out_shape=[
            shape((PAIRS, 2, BW, BW)),
            shape((2, BW, BW)),
            shape((2, SLAB_ORBITALS, BLK)),
        ],
        in_specs=whole(2),
        out_specs=whole(3),
        scratch_shapes=[pltpu.VMEM((3, SLAB_ORBITALS, SLAB_ORBITALS), bf16)],
        compiler_params=pltpu.CompilerParams(vmem_limit_bytes=VMEM_LIMIT),
    )(green, sigma)


def final_terms(*operands):
    return pl.pallas_call(
        final_kernel,
        out_shape=[shape((2, SLAB_ORBITALS, BLK)), shape((2, SLAB_ORBITALS, BLK))],
        in_specs=whole(len(operands)),
        out_specs=whole(2),
        scratch_shapes=[
            pltpu.VMEM((3, SLAB_ORBITALS, BW), bf16),
            pltpu.VMEM((3, SLAB_ORBITALS, BW), bf16),
            pltpu.VMEM((SLAB_ORBITALS, 2 * BW), bf16),
        ],
        compiler_params=pltpu.CompilerParams(vmem_limit_bytes=VMEM_LIMIT),
    )(*operands)


def dense_coupling(block_index, block_values):
    positions = jnp.arange(NBW, dtype=jnp.int32)[None, :]
    row_select = (block_index[:, 0:1] == positions).astype(jnp.float32)
    column_select = (block_index[:, 1:2] == positions).astype(jnp.float32)
    dense = jnp.einsum(
        "br,bc,bij->ricj", row_select, column_select, block_values, precision=FULL_PRECISION
    )
    return dense.reshape(BW, BW)


def partner_weights(targets, sources, phonon_shift, phonon_weight):
    target_column = jnp.asarray(targets)[..., None]
    source_column = jnp.asarray(sources)[..., None]
    emission = jnp.where(source_column == target_column + phonon_shift, phonon_weight[0], 0.0)
    absorption = jnp.where(source_column == target_column - phonon_shift, phonon_weight[1], 0.0)
    return jnp.sum(emission + absorption, axis=-1)


def body(green_ret, prev_lesser, coupling_index, coupling_values, phonon_shift, phonon_weight):
    green = green_ret[0, 0]
    coupling = dense_coupling(coupling_index[0], coupling_values[0])
    coupling_t = coupling.T
    lead, tail = slice(0, BW), slice(SLAB_ORBITALS - BW, SLAB_ORBITALS)
    g_ll, g_rl, g_lr = green[:, lead, lead], green[:, tail, lead], green[:, lead, tail]

    energy = lax.axis_index("energy")
    flipped = energy + 2 - 4 * (energy // 2 % 2)
    sources = jnp.stack([energy, energy ^ 1, flipped, flipped ^ 1]).astype(jnp.int32)
    targets = (energy + 4 * jnp.arange(4, dtype=jnp.int32)) % 16
    weights = partner_weights(targets[:, None], sources[None, :], phonon_shift, phonon_weight).reshape(16)

    sigma, transfer, inward, corner = phonon(
        weights, prev_lesser.reshape(STACKED, BLK), g_rl, g_lr, g_ll, coupling, coupling_t
    )
    outer_right, outer_left, outer_blocks = local_terms(green, sigma.reshape(2, SLAB_ORBITALS, BLK))
    state, retarded_far, lesser_far = sweep(
        transfer, inward, corner, coupling, coupling_t, g_ll, g_rl,
        outer_right[PAIRS - 1], outer_right[0], outer_left,
    )
    retarded, lesser = final_terms(green, state, retarded_far, lesser_far, outer_right, outer_blocks)
    return retarded[None, None], lesser[None, None]


def solution(mesh):
    placed = (
        P("slab", "energy", None, None, None),
        P("slab", "energy", None, None, None),
        P("slab", None, None),
        P("slab", None, None, None),
        P(),
        P(),
    )
    return jax.shard_map(
        body,
        mesh=mesh,
        in_specs=placed,
        out_specs=(P("slab", "energy", None, None, None), P("slab", "energy", None, None, None)),
        check_vma=False,
    )
```

```python
import functools

import jax
import jax.numpy as jnp
from jax import lax
from jax.experimental import pallas as pl
from jax.experimental.pallas import tpu as pltpu
from jax.sharding import PartitionSpec as P

SLAB_ORBITALS = 1536
BW = 256
BLK = 128
NBLK = 12
NBW = 2
PAIRS = SLAB_ORBITALS // BW
HALF = 4

FULL_PRECISION = lax.Precision.HIGHEST
MESH = pl.DeviceIdType.MESH
VMEM_LIMIT = 58 * 1024 * 1024
NN = (((1,), (0,)), ((), ()))
NT = (((1,), (1,)), ((), ()))

f32 = jnp.float32
bf16 = jnp.bfloat16


def dot(left, right, dims=NN):
    return lax.dot_general(left, right, dims, preferred_element_type=f32)


def split(value):
    high = value.astype(bf16)
    return high, (value - high.astype(f32)).astype(bf16)


def turned(value):
    width = value.shape[1] // 2
    return jnp.concatenate([-value[:, width:], value[:, :width]], axis=1)


def doubled(value):
    return jnp.concatenate([value, turned(value)], axis=0)


def product(left, right, dims=NN):
    left_high, left_low = split(left)
    right_high, right_low = split(right)
    main = doubled(right_high)
    return (
        dot(left_high, main, dims) + dot(left_low, main, dims) + dot(left_high, doubled(right_low), dims)
    )


def real_left(matrix, value):
    matrix_high, matrix_low = split(matrix)
    value_high, value_low = split(value)
    return dot(matrix_high, value_high) + dot(matrix_high, value_low) + dot(matrix_low, value_high)


def real_right(value, matrix):
    matrix_high, matrix_low = split(matrix)
    parts = []
    for part in (value[:, :BW], value[:, BW:]):
        high, low = split(part)
        parts.append(dot(high, matrix_high) + dot(low, matrix_high) + dot(high, matrix_low))
    return jnp.concatenate(parts, axis=1)


def beside(ref):
    return jnp.concatenate([ref[0], ref[1]], axis=1)


def adjoint(value):
    return jnp.concatenate([value[:, :BW].T, -value[:, BW:].T], axis=1)


class Place:
    def __init__(self):
        slab, energy = lax.axis_index("slab"), lax.axis_index("energy")
        self.half = slab // HALF
        self.z = slab % HALF
        base = self.half * HALF
        self.right = {"slab": base + (self.z + 1) % HALF}
        self.left = {"slab": base + (self.z + HALF - 1) % HALF}
        self.away = [{"slab": base + (self.z + d) % HALF} for d in (1, 2, 3)]
        other_half = (slab + HALF) % (2 * HALF)
        flipped = energy + 2 - 4 * (energy // 2 % 2)
        self.across = {"slab": other_half}
        self.across_flipped = {"slab": other_half, "energy": flipped}
        self.core = {"energy": energy + 1 - 2 * (energy % 2)}
        self.x_next = {"energy": (energy + 4) % 16}
        self.x_before = {"energy": (energy + 12) % 16}


def enter(others):
    barrier = pltpu.get_barrier_semaphore()
    for other in others:
        pl.semaphore_signal(barrier, inc=1, device_id=other, device_id_type=MESH)
    pl.semaphore_wait(barrier, len(others))


def sending(source, target, send, recv, device):
    return pltpu.make_async_remote_copy(
        src_ref=source, dst_ref=target, send_sem=send, recv_sem=recv, device_id=device, device_id_type=MESH
    )


class Gather:
    def __init__(self, place, slots, send, recv):
        z = place.z
        low, high = pl.ds(0, BW // 2), pl.ds(BW // 2, BW // 2)
        before, after, opposite = (z + 3) % HALF, (z + 1) % HALF, (z + 2) % HALF

        def copy(index, slot, rows, target):
            part = slots.at[slot, rows]
            return sending(part, part, send.at[index], recv.at[index], target)

        self.first = [
            copy(0, z, low, place.right),
            copy(1, z, high, place.left),
            copy(2, z, high, place.right),
            copy(3, z, low, place.left),
        ]
        self.arrive = [
            copy(0, before, low, place.right),
            copy(1, after, high, place.left),
            copy(2, before, high, place.right),
            copy(3, after, low, place.left),
        ]
        self.relay = [copy(4, before, low, place.right), copy(5, after, high, place.left)]
        self.last = [copy(4, opposite, low, place.right), copy(5, opposite, high, place.left)]

    def start(self):
        for item in self.first:
            item.start()

    def forward(self):
        for index in (0, 1):
            self.arrive[index].wait_recv()
            self.relay[index].start()

    def finish(self):
        for item in self.arrive[2:] + self.last:
            item.wait_recv()
        for item in self.first + self.relay:
            item.wait_send()


CHUNKS = 6
ROWS = SLAB_ORBITALS // CHUNKS
QUARTER = BW // HALF


def unit():
    row = lax.broadcasted_iota(jnp.int32, WIDE, 0)
    column = lax.broadcasted_iota(jnp.int32, WIDE, 1)
    return (row == column).astype(f32)


def phonon_kernel(
    weights, previous, g_rl, g_lr, g_ll, coupling, coupling_t,
    sigma, transfer, inward, corner, retarded, reach,
    others, relay, two_away, after, before, passing, from_before, from_after, mine,
    run, incoming,
    z_send, z_recv, y_send, y_recv, core_send, core_recv, x_send, x_recv, cross_send, cross_recv,
):
    place = Place()
    enter([place.left, place.right, place.across, place.across_flipped, place.core, place.x_next, place.x_before])
    z, half = place.z, place.half
    steps = range(CHUNKS)

    def rows(c):
        return pl.ds(c * ROWS, ROWS)

    def part(ref, index):
        return lambda c: ref.at[index, rows(c)]

    def both(ref):
        return lambda c: ref.at[:, rows(c)]

    def copies(sems, kind, source, target, device):
        send, recv = sems
        return [sending(source(c), target(c), send.at[kind, c], recv.at[kind, c], device) for c in steps]

    y, core, x = (y_send, y_recv), (core_send, core_recv), (x_send, x_recv)
    hop_a = copies(y, 0, part(previous, 0), part(relay, 0), place.across)
    end_a = copies(y, 1, part(relay, 0), part(others.at[1], 0), place.across_flipped)
    hop_b = copies(y, 2, part(previous, 1), part(relay, 1), place.across_flipped)
    end_b = copies(y, 3, part(relay, 1), part(others.at[1], 1), place.across)
    core_own = copies(core, 0, both(previous), both(others.at[0]), place.core)
    core_more = copies(core, 1, both(others.at[1]), both(others.at[2]), place.core)
    two_low = copies(x, 0, part(two_away, 0), part(passing, 0), place.x_next)
    two_high = copies(x, 1, part(two_away, 1), part(passing, 1), place.x_before)
    after_high = copies(x, 2, part(after, 1), part(from_before, 1), place.x_next)
    before_low = copies(x, 3, part(before, 0), part(from_after, 0), place.x_before)
    after_low = copies(x, 4, part(after, 0), part(from_before, 0), place.x_next)
    before_high = copies(x, 5, part(before, 1), part(from_after, 1), place.x_before)

    for c in (0, 1):
        hop_a[c].start()
        hop_b[c].start()
    for c in steps:
        core_own[c].start()

    turn = [Gather(place, ref, z_send.at[i], z_recv.at[i]) for i, ref in enumerate((transfer, inward, corner))]
    c_high, c_low = split(coupling[...])
    t_high, t_low = split(coupling_t[...])
    value = beside(g_rl)
    transfer[z] = dot(t_high, value) + dot(t_low, value)
    turn[0].start()
    parts = [dot(g_lr[i], c_high) + dot(g_lr[i], c_low) for i in (0, 1)]
    inward[z] = jnp.concatenate(parts, axis=1)
    corner[z] = beside(g_ll).astype(f32)

    def pass_on(c):
        hop_a[c].wait_recv()
        end_a[c].start()
        hop_b[c].wait_recv()
        end_b[c].start()
        if c + 2 < CHUNKS:
            hop_a[c + 2].start()
            hop_b[c + 2].start()

    def weigh(c):
        end_a[c].wait_recv()
        end_b[c].wait_recv()
        core_more[c].start()
        core_own[c].wait_recv()
        core_more[c].wait_recv()
        pieces = [previous[:, rows(c)]] + [others[i, :, rows(c)] for i in (0, 1, 2)]

        def weighted(target):
            total = weights[4 * target] * pieces[0]
            for source in (1, 2, 3):
                total = total + weights[4 * target + source] * pieces[source]
            return total

        two_away[:, rows(c)] = weighted(2)
        two_low[c].start()
        two_high[c].start()
        after[:, rows(c)] = weighted(1)
        after_high[c].start()
        before[:, rows(c)] = weighted(3)
        before_low[c].start()
        mine[:, rows(c)] = weighted(0)

    def add_passing(c):
        two_low[c].wait_recv()
        after[0, rows(c)] = after[0, rows(c)] + passing[0, rows(c)]
        after_low[c].start()
        two_high[c].wait_recv()
        before[1, rows(c)] = before[1, rows(c)] + passing[1, rows(c)]
        before_high[c].start()

    def finish(c):
        for item in (after_high, before_low, after_low, before_high):
            item[c].wait_recv()
        sigma[:, rows(c)] = (mine[:, rows(c)] + from_before[:, rows(c)] + from_after[:, rows(c)]).astype(bf16)

    over = sending(run, incoming, cross_send, cross_recv, place.across)

    def retarded_step(index, _):
        j = HALF - 1 - index

        @pl.when(j == z)
        def _():
            retarded[...] = run[...]

        run[...] = corner[j] + product(product(inward[j], run[...]), transfer[j])
        return 0

    def upper_corners():
        reach[...] = unit()

        @pl.when(half == 1)
        def _():
            retarded[...] = jnp.zeros_like(retarded)
            run[...] = corner[HALF - 1]
            lax.fori_loop(1, HALF, retarded_step, 0)
            over.start()

            def step(index, _):
                reach[...] = product(inward[z - 1 - index], reach[...])
                return 0

            lax.fori_loop(0, z, step, 0)

        @pl.when(half == 0)
        def _():
            def step(j, _):
                reach[...] = product(transfer[j], reach[...])
                return 0

            lax.fori_loop(z + 1, HALF, step, 0)

    for t in range(CHUNKS + 3):
        if t < CHUNKS:
            pass_on(t)
        if 0 <= t - 1 < CHUNKS:
            weigh(t - 1)
        if t in (1, 3, 5):
            turn[t // 2].forward()
            if t < 5:
                turn[t // 2 + 1].start()
        if 0 <= t - 2 < CHUNKS:
            add_passing(t - 2)
        if 0 <= t - 3 < CHUNKS:
            finish(t - 3)
        if t == CHUNKS + 1:
            for item in turn:
                item.finish()
            upper_corners()

    @pl.when(half == 0)
    def _():
        over.wait_recv()
        retarded[...] = incoming[...]

    @pl.when(half == 1)
    def _():
        over.wait_send()

    for group in (
        hop_a, end_a, hop_b, end_b, core_own, core_more,
        two_low, two_high, after_high, before_low, after_low, before_high,
    ):
        for item in group:
            item.wait_send()


class Shipment:
    def __init__(self, place, term, parts, quarter, total, send, recv):
        z = place.z

        def rows(index):
            return pl.ds(pl.multiple_of((index % HALF) * QUARTER, QUARTER), QUARTER)

        self.term, self.parts, self.quarter, self.here = term, parts, quarter, rows(z)
        self.spread = [
            sending(term.at[rows(z + d)], parts.at[d - 1], send.at[d - 1], recv.at[d - 1], place.away[d - 1])
            for d in (1, 2, 3)
        ]
        self.cross = sending(quarter, total.at[rows(z)], send.at[3], recv.at[3], place.across)
        self.hand = [
            sending(total.at[rows(z)], total.at[rows(z)], send.at[3 + d], recv.at[3 + d], place.away[d - 1])
            for d in (1, 2, 3)
        ]
        self.get = [
            sending(total.at[rows(z - d)], total.at[rows(z - d)], send.at[3 + d], recv.at[3 + d], place.away[d - 1])
            for d in (1, 2, 3)
        ]

    def start(self):
        for item in self.spread:
            item.start()

    def pass_over(self):
        for item in self.spread:
            item.wait_recv()
        self.quarter[...] = self.term[self.here, :] + self.parts[0] + self.parts[1] + self.parts[2]
        self.cross.start()

    def hand_on(self):
        self.cross.wait_recv()
        for item in self.hand:
            item.start()

    def arrive(self):
        for item in self.get:
            item.wait_recv()

    def sent(self):
        for item in self.spread + [self.cross]:
            item.wait_send()

    def handed(self):
        for item in self.hand:
            item.wait_send()


def sweep_kernel(
    transfer, inward, corner, retarded, reach, coupling, coupling_t, g_ll, g_rl, outer_rr, outer_rl, outer_ll,
    green_hbm, outer_right, outer_blocks,
    lesser_far, retarded_part, lesser_part,
    green, source, driven, own, through, term, parts, quarter, total, coupled, weighted,
    send, recv, ship_send, ship_recv, load,
):
    place = Place()
    z, half = place.z, place.half
    fetch = pltpu.make_async_copy(green_hbm, green, load)
    fetch.start()
    enter(place.away + [place.across])
    ship = Shipment(place, term, parts, quarter, total, ship_send, ship_recv)
    left, last = pl.ds(0, BW), pl.ds(SLAB_ORBITALS - BW, BW)
    stripe = 512

    def congruence(factor, value):
        return product(product(factor, value), factor, NT)

    turn = Gather(place, source, send.at[0], recv.at[0])
    source[z] = real_left(coupling_t[...], real_right(beside(outer_rr), coupling[...]))

    @pl.when(half == 0)
    def _():
        term[...] = congruence(reach[...], source[z])
        ship.start()

    turn.start()

    @pl.when(half == 0)
    def _():
        ship.pass_over()

    turn.forward()

    own[...] = retarded[...]

    def retarded_step(index, _):
        j = HALF - 1 - index
        own[...] = corner[j] + product(product(inward[j], own[...]), transfer[j])
        return 0

    @pl.when(half == 0)
    def _():
        lax.fori_loop(0, HALF - 1 - z, retarded_step, 0)

    def use_retarded():
        outer = real_right(own[...], coupling_t[...])
        through[...] = product(inward[z], outer)
        factor = doubled(real_left(coupling[...], outer).astype(bf16))
        fetch.wait()
        for start in range(0, SLAB_ORBITALS, stripe):
            span = pl.ds(start, stripe)
            piece = jnp.concatenate([green[0, span, last], green[1, span, last]], axis=1)
            weighted[span, :] = dot(piece, factor).astype(bf16)

        def pair(m, _):
            span = pl.ds(pl.multiple_of(m * BW, BW), BW)
            result = dot(
                weighted[span, :], doubled(jnp.concatenate([green[0, last, span], green[1, last, span]], axis=1))
            )
            for k in (0, 1):
                block = pl.ds(pl.multiple_of(m * BW + k * BLK, BLK), BLK)
                here = slice(k * BLK, (k + 1) * BLK)
                for i in (0, 1):
                    there = slice(i * BW + k * BLK, i * BW + (k + 1) * BLK)
                    retarded_part[i, block, :] = green[i, block, block].astype(f32) + result[here, there]
            return 0

        lax.fori_loop(0, PAIRS, pair, 0)

    use_retarded()

    @pl.when(half == 1)
    def _():
        ship.hand_on()

    turn.finish()
    own[...] = jnp.zeros_like(own)

    def forward_step(j, _):
        own[...] = congruence(transfer[j], own[...]) + source[j]
        return 0

    @pl.when(half == 0)
    def _():
        @pl.when(z > 0)
        def _():
            own[...] = source[0]

        lax.fori_loop(1, z, forward_step, 0)

    @pl.when(half == 1)
    def _():
        ship.arrive()
        own[...] = total[...]
        lax.fori_loop(0, z, forward_step, 0)

    state = doubled(own[...].astype(bf16))
    corner_l = beside(g_ll)
    near = dot(jnp.concatenate([corner_l, beside(g_rl)], axis=0), state).astype(bf16)
    right = dot(near, doubled(corner_l), NT)
    mixed = product(through[...], beside(outer_rl) + right[BW:])
    turn = Gather(place, driven, send.at[1], recv.at[1])
    driven[z] = beside(outer_ll) + right[:BW] + mixed + adjoint(mixed)

    @pl.when(half == 1)
    def _():
        term[...] = congruence(reach[...], driven[z])
        ship.start()

    turn.start()

    @pl.when(half == 1)
    def _():
        ship.pass_over()

    turn.forward()

    for start in range(0, SLAB_ORBITALS, stripe):
        span = pl.ds(start, stripe)
        piece = jnp.concatenate([green[0, span, left], green[1, span, left]], axis=1)
        result = dot(piece, state).astype(bf16)
        coupled[0, span, :] = result[:, :BW]
        coupled[1, span, :] = result[:, BW:]
        coupled[2, span, :] = -result[:, :BW]

    def against(left_rows, right_rows):
        first = coupled[0:2, left_rows, :].reshape(2 * BW, BW)
        second = coupled[1:3, left_rows, :].reshape(2 * BW, BW)
        result = dot(first, green[0, right_rows, left], NT) + dot(second, green[1, right_rows, left], NT)
        return result.reshape(2, BW, BW)

    def pair(m, _):
        span = pl.ds(pl.multiple_of(m * BW, BW), BW)
        far_right = (outer_right[m] + against(last, span)).astype(bf16)
        mixed = dot(weighted[span, :], doubled(jnp.concatenate([far_right[0], far_right[1]], axis=1)))
        local = against(span, span)
        for k in (0, 1):
            block = pl.ds(pl.multiple_of(m * BW + k * BLK, BLK), BLK)
            here = slice(k * BLK, (k + 1) * BLK)
            for i in (0, 1):
                there = slice(i * BW + k * BLK, i * BW + (k + 1) * BLK)
                mix = mixed[here, there]
                mirrored = mix.T if i == 0 else -mix.T
                lesser_part[i, block, :] = outer_blocks[i, block, :] + local[i, here, here] + mix + mirrored
        return 0

    lax.fori_loop(0, PAIRS, pair, 0)

    @pl.when(half == 0)
    def _():
        ship.hand_on()

    turn.finish()
    own[...] = jnp.zeros_like(own)

    def backward_step(index, _):
        j = HALF - 1 - index
        own[...] = congruence(inward[j], own[...]) + driven[j]
        return 0

    @pl.when(half == 1)
    def _():
        @pl.when(z < HALF - 1)
        def _():
            own[...] = driven[HALF - 1]

        lax.fori_loop(1, HALF - 1 - z, backward_step, 0)

    @pl.when(half == 0)
    def _():
        ship.arrive()
        own[...] = total[...]
        lax.fori_loop(0, HALF - 1 - z, backward_step, 0)

    lesser_far[...] = real_left(coupling[...], real_right(own[...], coupling_t[...])).astype(bf16)
    ship.sent()
    ship.handed()


def local_kernel(green, sigma, outer_right, outer_rr, outer_rl, outer_left, outer_blocks, scaled):
    rows = 512

    def scale(n, _):
        columns = pl.ds(pl.multiple_of(n * BLK, BLK), BLK)
        real, imag = sigma[0, columns, :], sigma[1, columns, :]
        factor = jnp.concatenate(
            [jnp.concatenate([real, imag], axis=1), jnp.concatenate([-imag, real], axis=1)], axis=0
        )
        for start in range(0, SLAB_ORBITALS, rows):
            span = pl.ds(start, rows)
            piece = jnp.concatenate([green[0, span, columns], green[1, span, columns]], axis=1)
            result = dot(piece, factor).astype(bf16)
            scaled[0, span, columns] = result[:, :BLK]
            scaled[1, span, columns] = result[:, BLK:]
            scaled[2, span, columns] = -result[:, :BLK]
        return 0

    lax.fori_loop(0, NBLK, scale, 0)
    last = pl.ds(SLAB_ORBITALS - BW, BW)

    def against(left_rows, right_rows):
        first = scaled[0:2, left_rows, :].reshape(2 * BW, SLAB_ORBITALS)
        second = scaled[1:3, left_rows, :].reshape(2 * BW, SLAB_ORBITALS)
        total = dot(first, green[0, right_rows, :], NT) + dot(second, green[1, right_rows, :], NT)
        return total.reshape(2, BW, BW)

    def pair(m, _):
        span = pl.ds(pl.multiple_of(m * BW, BW), BW)
        far = against(last, span)
        outer_right[m] = far
        local = against(span, span)
        first = pl.ds(pl.multiple_of(m * BW, BW), BLK)
        second = pl.ds(pl.multiple_of(m * BW + BLK, BLK), BLK)
        outer_blocks[:, first, :] = local[:, :BLK, :BLK]
        outer_blocks[:, second, :] = local[:, BLK:, BLK:]

        @pl.when(m == 0)
        def _():
            outer_left[...] = local
            outer_rl[...] = far

        @pl.when(m == PAIRS - 1)
        def _():
            outer_rr[...] = far

        return 0

    lax.fori_loop(0, PAIRS, pair, 0)


def final_kernel(green, lesser_far, retarded_part, lesser_part, retarded_out, lesser_out):
    right = jnp.concatenate([green[0], green[1]], axis=1)
    weighted = dot(right, doubled(lesser_far[...])).astype(bf16)
    real, imag = weighted[:, :BW], weighted[:, BW:]
    first = jnp.concatenate([real, imag], axis=0)
    second = jnp.concatenate([imag, -real], axis=0)
    total = dot(first, green[0], NT) + dot(second, green[1], NT)
    retarded_out[...] = retarded_part[...]
    for k in (0, 1):
        block = slice(k * BLK, (k + 1) * BLK)
        for i in (0, 1):
            here = slice(i * BW + k * BLK, i * BW + (k + 1) * BLK)
            lesser_out[i, block, :] = lesser_part[i, block, :] + total[here, block]


def whole(count):
    return [pl.BlockSpec(memory_space=pltpu.VMEM)] * count


def shape(dims, dtype=f32):
    return jax.ShapeDtypeStruct(dims, dtype)


WIDE = (BW, 2 * BW)


def phonon(weights, previous, *operands):
    stacked = pltpu.VMEM((2, SLAB_ORBITALS, BLK), f32)
    dma = pltpu.SemaphoreType.DMA
    return pl.pallas_call(
        phonon_kernel,
        out_shape=[shape((2, SLAB_ORBITALS, BLK), bf16)] + [shape((HALF,) + WIDE)] * 3 + [shape(WIDE)] * 2,
        in_specs=[pl.BlockSpec(memory_space=pltpu.SMEM)] + whole(1 + len(operands)),
        out_specs=whole(6),
        scratch_shapes=[pltpu.VMEM((3, 2, SLAB_ORBITALS, BLK), f32)]
        + [stacked] * 8
        + [pltpu.VMEM(WIDE, f32)] * 2
        + [
            dma((3, 6)),
            dma((3, 6)),
            dma((4, CHUNKS)),
            dma((4, CHUNKS)),
            dma((2, CHUNKS)),
            dma((2, CHUNKS)),
            dma((6, CHUNKS)),
            dma((6, CHUNKS)),
            dma,
            dma,
        ],
        compiler_params=pltpu.CompilerParams(
            collective_id=0, has_side_effects=True, vmem_limit_bytes=VMEM_LIMIT
        ),
    )(weights, previous, *operands)


def sweep(green, *operands):
    wide = pltpu.VMEM(WIDE, f32)
    dma = pltpu.SemaphoreType.DMA
    specs = whole(len(operands) + 1)
    specs[12] = pl.BlockSpec(memory_space=pl.ANY)
    return pl.pallas_call(
        sweep_kernel,
        out_shape=[shape(WIDE, bf16)] + [shape((2, SLAB_ORBITALS, BLK))] * 2,
        in_specs=specs,
        out_specs=whole(3),
        scratch_shapes=[
            pltpu.VMEM((2, SLAB_ORBITALS, SLAB_ORBITALS), bf16),
            pltpu.VMEM((HALF,) + WIDE, f32),
            pltpu.VMEM((HALF,) + WIDE, f32),
            wide,
            wide,
            wide,
            pltpu.VMEM((3, QUARTER, 2 * BW), f32),
            pltpu.VMEM((QUARTER, 2 * BW), f32),
            wide,
            pltpu.VMEM((3, SLAB_ORBITALS, BW), bf16),
            pltpu.VMEM((SLAB_ORBITALS, 2 * BW), bf16),
            dma((2, 6)),
            dma((2, 6)),
            dma((7,)),
            dma((7,)),
            dma,
        ],
        compiler_params=pltpu.CompilerParams(
            collective_id=1, has_side_effects=True, vmem_limit_bytes=VMEM_LIMIT
        ),
    )(*operands[:12], green, *operands[12:])


def local_terms(green, sigma):
    return pl.pallas_call(
        local_kernel,
        out_shape=[
            shape((PAIRS, 2, BW, BW)),
            shape((2, BW, BW)),
            shape((2, BW, BW)),
            shape((2, BW, BW)),
            shape((2, SLAB_ORBITALS, BLK)),
        ],
        in_specs=whole(2),
        out_specs=whole(5),
        scratch_shapes=[pltpu.VMEM((3, SLAB_ORBITALS, SLAB_ORBITALS), bf16)],
        compiler_params=pltpu.CompilerParams(vmem_limit_bytes=VMEM_LIMIT),
    )(green, sigma)


def final_terms(*operands):
    strip = pl.BlockSpec((2, BW, BLK), lambda m: (0, m, 0))
    return pl.pallas_call(
        final_kernel,
        grid=(PAIRS,),
        out_shape=[shape((2, SLAB_ORBITALS, BLK))] * 2,
        in_specs=[
            pl.BlockSpec((2, BW, BW), lambda m: (0, m, PAIRS - 1)),
            pl.BlockSpec(WIDE, lambda m: (0, 0)),
            strip,
            strip,
        ],
        out_specs=[strip, strip],
        compiler_params=pltpu.CompilerParams(vmem_limit_bytes=VMEM_LIMIT),
    )(*operands)


def dense_coupling(block_index, block_values):
    positions = jnp.arange(NBW, dtype=jnp.int32)[None, :]
    row_select = (block_index[:, 0:1] == positions).astype(jnp.float32)
    column_select = (block_index[:, 1:2] == positions).astype(jnp.float32)
    dense = jnp.einsum(
        "br,bc,bij->ricj", row_select, column_select, block_values, precision=FULL_PRECISION
    )
    return dense.reshape(BW, BW)


def partner_weights(targets, sources, phonon_shift, phonon_weight):
    target_column = jnp.asarray(targets)[..., None]
    source_column = jnp.asarray(sources)[..., None]
    emission = jnp.where(source_column == target_column + phonon_shift, phonon_weight[0], 0.0)
    absorption = jnp.where(source_column == target_column - phonon_shift, phonon_weight[1], 0.0)
    return jnp.sum(emission + absorption, axis=-1)


def body(green_ret, prev_lesser, coupling_index, coupling_values, phonon_shift, phonon_weight):
    green = green_ret[0, 0]
    coupling = dense_coupling(coupling_index[0], coupling_values[0])
    coupling_t = coupling.T
    lead, tail = slice(0, BW), slice(SLAB_ORBITALS - BW, SLAB_ORBITALS)
    g_ll, g_rl, g_lr = green[:, lead, lead], green[:, tail, lead], green[:, lead, tail]

    energy = lax.axis_index("energy")
    flipped = energy + 2 - 4 * (energy // 2 % 2)
    sources = jnp.stack([energy, energy ^ 1, flipped, flipped ^ 1]).astype(jnp.int32)
    targets = (energy + 4 * jnp.arange(4, dtype=jnp.int32)) % 16
    weights = partner_weights(targets[:, None], sources[None, :], phonon_shift, phonon_weight).reshape(16)

    sigma, transfer, inward, corner, retarded, reach = phonon(
        weights, prev_lesser[0, 0], g_rl, g_lr, g_ll, coupling, coupling_t
    )
    outer_right, outer_rr, outer_rl, outer_left, outer_blocks = local_terms(green, sigma)
    lesser_far, retarded_part, lesser_part = sweep(
        green, transfer, inward, corner, retarded, reach, coupling, coupling_t, g_ll, g_rl,
        outer_rr, outer_rl, outer_left, outer_right, outer_blocks,
    )
    retarded, lesser = final_terms(green, lesser_far, retarded_part, lesser_part)
    return retarded[None, None], lesser[None, None]


def solution(mesh):
    placed = (
        P("slab", "energy", None, None, None),
        P("slab", "energy", None, None, None),
        P("slab", None, None),
        P("slab", None, None, None),
        P(),
        P(),
    )
    return jax.shard_map(
        body,
        mesh=mesh,
        in_specs=placed,
        out_specs=(P("slab", "energy", None, None, None), P("slab", "energy", None, None, None)),
        check_vma=False,
    )
```

```python
import functools

import jax
import jax.numpy as jnp
from jax import lax
from jax.experimental import pallas as pl
from jax.experimental.pallas import tpu as pltpu
from jax.sharding import PartitionSpec as P

SLAB_ORBITALS = 1536
BW = 256
BLK = 128
NBLK = 12
NBW = 2
NMODE = 3
NNZ = 3
PAIRS = SLAB_ORBITALS // BW
HALF = 4

MESH = pl.DeviceIdType.MESH
VMEM_LIMIT = 61 * 1024 * 1024
NN = (((1,), (0,)), ((), ()))
NT = (((1,), (1,)), ((), ()))

f32 = jnp.float32
bf16 = jnp.bfloat16


def dot(left, right, dims=NN):
    return lax.dot_general(left, right, dims, preferred_element_type=f32)


def split(value):
    high = value.astype(bf16)
    return high, (value - high.astype(f32)).astype(bf16)


def turned(value):
    width = value.shape[1] // 2
    return jnp.concatenate([-value[:, width:], value[:, :width]], axis=1)


def doubled(value):
    return jnp.concatenate([value, turned(value)], axis=0)


def product(left, right, dims=NN):
    left_high, left_low = split(left)
    right_high, right_low = split(right)
    main = doubled(right_high)
    return (
        dot(left_high, main, dims) + dot(left_low, main, dims) + dot(left_high, doubled(right_low), dims)
    )


def real_left(matrix, value):
    matrix_high, matrix_low = split(matrix)
    value_high, value_low = split(value)
    return dot(matrix_high, value_high) + dot(matrix_high, value_low) + dot(matrix_low, value_high)


def real_right(value, matrix):
    matrix_high, matrix_low = split(matrix)
    parts = []
    for part in (value[:, :BW], value[:, BW:]):
        high, low = split(part)
        parts.append(dot(high, matrix_high) + dot(low, matrix_high) + dot(high, matrix_low))
    return jnp.concatenate(parts, axis=1)


def beside(ref):
    return jnp.concatenate([ref[0], ref[1]], axis=1)


def adjoint(value):
    return jnp.concatenate([value[:, :BW].T, -value[:, BW:].T], axis=1)


class Place:
    def __init__(self):
        slab, energy = lax.axis_index("slab"), lax.axis_index("energy")
        self.half = slab // HALF
        self.z = slab % HALF
        base = self.half * HALF
        self.right = {"slab": base + (self.z + 1) % HALF}
        self.left = {"slab": base + (self.z + HALF - 1) % HALF}
        self.away = [{"slab": base + (self.z + d) % HALF} for d in (1, 2, 3)]
        other_half = (slab + HALF) % (2 * HALF)
        flipped = energy + 2 - 4 * (energy // 2 % 2)
        self.across = {"slab": other_half}
        self.y_partner = {"energy": flipped}
        self.energy, self.flipped = energy, flipped
        self.core = {"energy": energy + 1 - 2 * (energy % 2)}
        self.x_next = {"energy": (energy + 4) % 16}
        self.x_before = {"energy": (energy + 12) % 16}


def enter(others):
    barrier = pltpu.get_barrier_semaphore()
    for other in others:
        pl.semaphore_signal(barrier, inc=1, device_id=other, device_id_type=MESH)
    pl.semaphore_wait(barrier, len(others))


def sending(source, target, send, recv, device):
    return pltpu.make_async_remote_copy(
        src_ref=source, dst_ref=target, send_sem=send, recv_sem=recv, device_id=device, device_id_type=MESH
    )


class Gather:
    def __init__(self, place, slots, send, recv):
        z = place.z
        low, high = pl.ds(0, BW // 2), pl.ds(BW // 2, BW // 2)
        before, after, opposite = (z + 3) % HALF, (z + 1) % HALF, (z + 2) % HALF

        def copy(index, slot, rows, target):
            part = slots.at[slot, rows]
            return sending(part, part, send.at[index], recv.at[index], target)

        self.first = [
            copy(0, z, low, place.right),
            copy(1, z, high, place.left),
            copy(2, z, high, place.right),
            copy(3, z, low, place.left),
        ]
        self.arrive = [
            copy(0, before, low, place.right),
            copy(1, after, high, place.left),
            copy(2, before, high, place.right),
            copy(3, after, low, place.left),
        ]
        self.relay = [copy(4, before, low, place.right), copy(5, after, high, place.left)]
        self.last = [copy(4, opposite, low, place.right), copy(5, opposite, high, place.left)]

    def start(self):
        for item in self.first:
            item.start()

    def forward(self):
        for index in (0, 1):
            self.arrive[index].wait_recv()
            self.relay[index].start()

    def finish(self):
        for item in self.arrive[2:] + self.last:
            item.wait_recv()
        for item in self.first + self.relay:
            item.wait_send()


CHUNKS = 6
ROWS = SLAB_ORBITALS // CHUNKS
QUARTER = BW // HALF
STRIPE = 512


def unit():
    row = lax.broadcasted_iota(jnp.int32, WIDE, 0)
    column = lax.broadcasted_iota(jnp.int32, WIDE, 1)
    return (row == column).astype(f32)


class Shipment:
    def __init__(self, place, term, parts, quarter, total, send, recv):
        z = place.z

        def rows(index):
            return pl.ds(pl.multiple_of((index % HALF) * QUARTER, QUARTER), QUARTER)

        self.term, self.parts, self.quarter, self.here = term, parts, quarter, rows(z)
        self.spread = [
            sending(term.at[rows(z + d)], parts.at[d - 1], send.at[d - 1], recv.at[d - 1], place.away[d - 1])
            for d in (1, 2, 3)
        ]
        self.cross = sending(quarter, total.at[rows(z)], send.at[3], recv.at[3], place.across)
        self.hand = [
            sending(total.at[rows(z)], total.at[rows(z)], send.at[3 + d], recv.at[3 + d], place.away[d - 1])
            for d in (1, 2, 3)
        ]
        self.get = [
            sending(total.at[rows(z - d)], total.at[rows(z - d)], send.at[3 + d], recv.at[3 + d], place.away[d - 1])
            for d in (1, 2, 3)
        ]

    def start(self):
        for item in self.spread:
            item.start()

    def pass_over(self):
        for item in self.spread:
            item.wait_recv()
        self.quarter[...] = self.term[self.here, :] + self.parts[0] + self.parts[1] + self.parts[2]
        self.cross.start()

    def hand_on(self):
        self.cross.wait_recv()
        for item in self.hand:
            item.start()

    def arrive(self):
        for item in self.get:
            item.wait_recv()

    def sent(self):
        for item in self.spread + [self.cross]:
            item.wait_send()

    def handed(self):
        for item in self.hand:
            item.wait_send()


def partner_weights(target, sources, shift, weight):
    result = []
    for source in sources:
        total = 0.0
        for mode in range(NMODE):
            total = total + jnp.where(source == target + shift[mode], weight[0, mode], 0.0)
            total = total + jnp.where(source == target - shift[mode], weight[1, mode], 0.0)
        result.append(total)
    return result


def dense_coupling(index, values, coupling, coupling_t):
    for row in range(NBW):
        for column in range(NBW):
            block = jnp.zeros((BLK, BLK), f32)
            for item in range(NNZ):
                here = (index[item, 0] == row) & (index[item, 1] == column)
                block = block + jnp.where(here, 1.0, 0.0) * values[item]
            rows, columns = pl.ds(row * BLK, BLK), pl.ds(column * BLK, BLK)
            coupling[rows, columns] = block
            coupling_t[columns, rows] = block.T


def sweep_kernel(
    shift, weight, index, values, previous, green_hbm,
    lesser_far, retarded_part, lesser_part,
    green, coupling, coupling_t, transfer, inward, corner,
    others, two_away, after, before, passing, from_before, from_after,
    scaled, outer_right, outer_left, source, driven, weighted,
    run, incoming, own, through, term, total, reach, near, parts, quarter,
    load, z_send, z_recv, y_send, y_recv, core_send, core_recv, x_send, x_recv,
    cross_send, cross_recv, ship_send, ship_recv,
):
    place = Place()
    z, half = place.z, place.half
    steps = range(CHUNKS)
    left, last = pl.ds(0, BW), pl.ds(SLAB_ORBITALS - BW, BW)
    middle = pl.ds(BW, SLAB_ORBITALS - 2 * BW)
    fetch = [
        pltpu.make_async_copy(green_hbm.at[:, span], green.at[:, span], load.at[i])
        for i, span in enumerate((last, left, middle))
    ]
    for item in fetch:
        item.start()
    enter(place.away + [place.across, place.y_partner, place.core, place.x_next, place.x_before])


    def rows(c):
        return pl.ds(c * ROWS, ROWS)

    def part(ref, i):
        return lambda c: ref.at[i, rows(c)]

    def both(ref):
        return lambda c: ref.at[:, rows(c)]

    def copies(sems, kind, origin, target, device):
        send, recv = sems
        return [sending(origin(c), target(c), send.at[kind, c], recv.at[kind, c], device) for c in steps]

    y, core, x = (y_send, y_recv), (core_send, core_recv), (x_send, x_recv)
    over_y = copies(y, 0, both(previous), both(others.at[1]), place.y_partner)
    core_own = copies(core, 0, both(previous), both(others.at[0]), place.core)
    core_more = copies(core, 1, both(others.at[1]), both(others.at[2]), place.core)
    two_low = copies(x, 0, part(two_away, 0), part(passing, 0), place.x_next)
    two_high = copies(x, 1, part(two_away, 1), part(passing, 1), place.x_before)
    after_high = copies(x, 2, part(after, 1), part(from_before, 1), place.x_next)
    before_low = copies(x, 3, part(before, 0), part(from_after, 0), place.x_before)
    after_low = copies(x, 4, part(after, 0), part(from_before, 0), place.x_next)
    before_high = copies(x, 5, part(before, 1), part(from_after, 1), place.x_before)

    for c in (0, 1):
        over_y[c].start()
    for c in steps:
        core_own[c].start()

    sources = [place.energy, place.energy + 1 - 2 * (place.energy % 2)]
    sources += [place.flipped, place.flipped + 1 - 2 * (place.flipped % 2)]
    weights = [partner_weights((place.energy + 4 * t) % 16, sources, shift, weight) for t in range(4)]
    dense_coupling(index, values, coupling, coupling_t)
    turn = [Gather(place, ref, z_send.at[i], z_recv.at[i]) for i, ref in enumerate((transfer, inward, corner))]

    def near_factors():
        t_high, t_low = split(coupling_t[...])
        fetch[0].wait()
        value = jnp.concatenate([green[0, last, left], green[1, last, left]], axis=1)
        transfer[z] = dot(t_high, value) + dot(t_low, value)
        turn[0].start()
        fetch[1].wait()
        c_high, c_low = split(coupling[...])
        halves = [dot(green[i, left, last], c_high) + dot(green[i, left, last], c_low) for i in (0, 1)]
        inward[z] = jnp.concatenate(halves, axis=1)
        corner[z] = jnp.concatenate([green[0, left, left], green[1, left, left]], axis=1).astype(f32)
        fetch[2].wait()

    def weigh(c):
        over_y[c].wait_recv()
        core_more[c].start()
        if c + 2 < CHUNKS:
            over_y[c + 2].start()
        core_own[c].wait_recv()
        core_more[c].wait_recv()
        pieces = [previous[:, rows(c)]] + [others[i, :, rows(c)] for i in (0, 1, 2)]

        def sums(target):
            result = weights[target][0] * pieces[0]
            for i in (1, 2, 3):
                result = result + weights[target][i] * pieces[i]
            return result

        two_away[:, rows(c)] = sums(2)
        two_low[c].start()
        two_high[c].start()
        after[:, rows(c)] = sums(1)
        after_high[c].start()
        before[:, rows(c)] = sums(3)
        before_low[c].start()

    def add_passing(c):
        two_low[c].wait_recv()
        after[0, rows(c)] = after[0, rows(c)] + passing[0, rows(c)]
        after_low[c].start()
        two_high[c].wait_recv()
        before[1, rows(c)] = before[1, rows(c)] + passing[1, rows(c)]
        before_high[c].start()

    def self_energy(c):
        mine = weights[0][0] * previous[:, rows(c)]
        for i in (0, 1, 2):
            mine = mine + weights[0][i + 1] * others[i, :, rows(c)]
        for item in (after_high, before_low, after_low, before_high):
            item[c].wait_recv()
        return (mine + from_before[:, rows(c)] + from_after[:, rows(c)]).astype(bf16)


    def against(values, left_rows, right_rows, columns):
        first = values[0:2, left_rows, :].reshape(2 * BW, BW)
        second = values[1:3, left_rows, :].reshape(2 * BW, BW)
        result = dot(first, green[0, right_rows, columns], NT) + dot(second, green[1, right_rows, columns], NT)
        return result.reshape(2, BW, BW)

    def keep(span, result):
        scaled[0, span[0], span[1]] = result[:, : result.shape[1] // 2]
        scaled[1, span[0], span[1]] = result[:, result.shape[1] // 2 :]
        scaled[2, span[0], span[1]] = -result[:, : result.shape[1] // 2]

    def local_terms(c):
        sigma = self_energy(c)
        for k in (0, 1):
            real, imag = sigma[0, k * BLK : (k + 1) * BLK], sigma[1, k * BLK : (k + 1) * BLK]
            factor = doubled(jnp.concatenate([real, imag], axis=1))
            columns = pl.ds(c * BW + k * BLK, BLK)
            for start in range(0, SLAB_ORBITALS, STRIPE):
                span = pl.ds(start, STRIPE)
                piece = jnp.concatenate([green[0, span, columns], green[1, span, columns]], axis=1)
                keep((span, pl.ds(k * BLK, BLK)), dot(piece, factor).astype(bf16))
        columns = pl.ds(c * BW, BW)

        def pair(m, _):
            span = pl.ds(pl.multiple_of(m * BW, BW), BW)
            far = against(scaled, last, span, columns)
            outer_right[m] = far if c == 0 else outer_right[m] + far
            local = against(scaled, span, span, columns)
            for k in (0, 1):
                block = pl.ds(pl.multiple_of(m * BW + k * BLK, BLK), BLK)
                here = slice(k * BLK, (k + 1) * BLK)
                value = local[:, here, here]
                lesser_part[:, block, :] = value if c == 0 else lesser_part[:, block, :] + value

            @pl.when(m == 0)
            def _():
                outer_left[...] = local if c == 0 else outer_left[...] + local

            return 0

        lax.fori_loop(0, PAIRS, pair, 0)

    def reaches():
        reach[...] = unit()
        near[...] = unit()

        def over_transfer(ref):
            def step(j, _):
                ref[...] = product(transfer[j], ref[...])
                return 0

            return step

        def over_inward(ref):
            def step(i, _):
                j = HALF - 1 - i
                ref[...] = product(inward[j], ref[...])
                return 0

            return step

        @pl.when(half == 0)
        def _():
            lax.fori_loop(z + 1, HALF, over_transfer(reach), 0)
            lax.fori_loop(0, HALF - 1 - z, over_inward(near), 0)

        @pl.when(half == 1)
        def _():
            lax.fori_loop(HALF - z, HALF, over_inward(reach), 0)
            lax.fori_loop(0, z, over_transfer(near), 0)

    for t in range(CHUNKS + 2):
        if t < CHUNKS:
            weigh(t)
        if t == 0:
            near_factors()
        if t in (1, 3, 5):
            turn[t // 2].forward()
            if t < 5:
                turn[t // 2 + 1].start()
        if 0 <= t - 1 < CHUNKS:
            add_passing(t - 1)
        if t == CHUNKS:
            turn[0].finish()
            turn[1].finish()
            reaches()
        if 0 <= t - 2 < CHUNKS:
            local_terms(t - 2)


    ship = Shipment(place, term, parts, quarter, total, ship_send, ship_recv)
    over = sending(run, incoming, cross_send, cross_recv, place.across)

    def congruence(factor, value):
        return product(product(factor, value), factor, NT)

    gather = Gather(place, source, z_send.at[3], z_recv.at[3])
    source[z] = real_left(coupling_t[...], real_right(beside(outer_right.at[PAIRS - 1]), coupling[...]))

    @pl.when(half == 0)
    def _():
        term[...] = congruence(reach[...], source[z])
        ship.start()

    gather.start()

    @pl.when(half == 0)
    def _():
        ship.pass_over()

    gather.forward()
    turn[2].finish()

    def retarded_step(i, _):
        j = HALF - 1 - i

        @pl.when(j == z)
        def _():
            own[...] = run[...]

        run[...] = corner[j] + product(product(inward[j], run[...]), transfer[j])
        return 0

    @pl.when(half == 1)
    def _():
        own[...] = jnp.zeros_like(own)
        run[...] = corner[HALF - 1]
        lax.fori_loop(1, HALF, retarded_step, 0)
        over.start()

    @pl.when(half == 0)
    def _():
        over.wait_recv()
        run[...] = incoming[...]
        lax.fori_loop(0, HALF - 1 - z, retarded_step, 0)
        own[...] = run[...]

    def use_retarded():
        outer = real_right(own[...], coupling_t[...])
        through[...] = product(inward[z], outer)
        factor = doubled(real_left(coupling[...], outer).astype(bf16))
        for start in range(0, SLAB_ORBITALS, STRIPE):
            span = pl.ds(start, STRIPE)
            piece = jnp.concatenate([green[0, span, last], green[1, span, last]], axis=1)
            weighted[span, :] = dot(piece, factor).astype(bf16)

        def pair(m, _):
            span = pl.ds(pl.multiple_of(m * BW, BW), BW)
            result = dot(
                weighted[span, :], doubled(jnp.concatenate([green[0, last, span], green[1, last, span]], axis=1))
            )
            for k in (0, 1):
                block = pl.ds(pl.multiple_of(m * BW + k * BLK, BLK), BLK)
                here = slice(k * BLK, (k + 1) * BLK)
                for i in (0, 1):
                    there = slice(i * BW + k * BLK, i * BW + (k + 1) * BLK)
                    retarded_part[i, block, :] = green[i, block, block].astype(f32) + result[here, there]
            return 0

        lax.fori_loop(0, PAIRS, pair, 0)

    use_retarded()

    @pl.when(half == 1)
    def _():
        ship.hand_on()

    gather.finish()
    own[...] = jnp.zeros_like(own)

    def forward_step(j, _):
        own[...] = congruence(transfer[j], own[...]) + source[j]
        return 0

    @pl.when(z > 0)
    def _():
        own[...] = source[0]

    lax.fori_loop(1, z, forward_step, 0)

    @pl.when(half == 1)
    def _():
        ship.arrive()
        own[...] = own[...] + congruence(near[...], total[...])

    state = doubled(own[...].astype(bf16))
    corner_l = jnp.concatenate([green[0, left, left], green[1, left, left]], axis=1)
    corner_rl = jnp.concatenate([green[0, last, left], green[1, last, left]], axis=1)
    edge = dot(jnp.concatenate([corner_l, corner_rl], axis=0), state).astype(bf16)
    right = dot(edge, doubled(corner_l), NT)
    mixed = product(through[...], beside(outer_right.at[0]) + right[BW:])
    gather = Gather(place, driven, z_send.at[4], z_recv.at[4])
    driven[z] = beside(outer_left) + right[:BW] + mixed + adjoint(mixed)

    @pl.when(half == 1)
    def _():
        term[...] = congruence(reach[...], driven[z])
        ship.start()

    gather.start()

    @pl.when(half == 1)
    def _():
        ship.pass_over()

    gather.forward()

    for start in range(0, SLAB_ORBITALS, STRIPE):
        span = pl.ds(start, STRIPE)
        piece = jnp.concatenate([green[0, span, left], green[1, span, left]], axis=1)
        keep((span, pl.ds(0, BW)), dot(piece, state).astype(bf16))

    def pair(m, _):
        span = pl.ds(pl.multiple_of(m * BW, BW), BW)
        far_right = (outer_right[m] + against(scaled, last, span, left)).astype(bf16)
        mixed = dot(weighted[span, :], doubled(jnp.concatenate([far_right[0], far_right[1]], axis=1)))
        local = against(scaled, span, span, left)
        for k in (0, 1):
            block = pl.ds(pl.multiple_of(m * BW + k * BLK, BLK), BLK)
            here = slice(k * BLK, (k + 1) * BLK)
            for i in (0, 1):
                there = slice(i * BW + k * BLK, i * BW + (k + 1) * BLK)
                mix = mixed[here, there]
                mirrored = mix.T if i == 0 else -mix.T
                lesser_part[i, block, :] = lesser_part[i, block, :] + local[i, here, here] + mix + mirrored
        return 0

    lax.fori_loop(0, PAIRS, pair, 0)

    @pl.when(half == 0)
    def _():
        ship.hand_on()

    gather.finish()
    own[...] = jnp.zeros_like(own)

    def backward_step(i, _):
        j = HALF - 1 - i
        own[...] = congruence(inward[j], own[...]) + driven[j]
        return 0

    @pl.when(z < HALF - 1)
    def _():
        own[...] = driven[HALF - 1]

    lax.fori_loop(1, HALF - 1 - z, backward_step, 0)

    @pl.when(half == 0)
    def _():
        ship.arrive()
        own[...] = own[...] + congruence(near[...], total[...])

    lesser_far[...] = real_left(coupling[...], real_right(own[...], coupling_t[...])).astype(bf16)
    ship.sent()
    ship.handed()

    @pl.when(half == 1)
    def _():
        over.wait_send()

    for group in (
        over_y, core_own, core_more, two_low, two_high, after_high, before_low, after_low, before_high,
    ):
        for item in group:
            item.wait_send()


def final_kernel(green, lesser_far, retarded_part, lesser_part, retarded_out, lesser_out):
    right = jnp.concatenate([green[0], green[1]], axis=1)
    weighted = dot(right, doubled(lesser_far[...])).astype(bf16)
    real, imag = weighted[:, :BW], weighted[:, BW:]
    first = jnp.concatenate([real, imag], axis=0)
    second = jnp.concatenate([imag, -real], axis=0)
    total = dot(first, green[0], NT) + dot(second, green[1], NT)
    retarded_out[...] = retarded_part[...]
    for k in (0, 1):
        block = slice(k * BLK, (k + 1) * BLK)
        for i in (0, 1):
            here = slice(i * BW + k * BLK, i * BW + (k + 1) * BLK)
            lesser_out[i, block, :] = lesser_part[i, block, :] + total[here, block]


def whole(count):
    return [pl.BlockSpec(memory_space=pltpu.VMEM)] * count


def shape(dims, dtype=f32):
    return jax.ShapeDtypeStruct(dims, dtype)


WIDE = (BW, 2 * BW)


def sweep(shift, weight, index, values, previous, green):
    def wide(count):
        return [pltpu.VMEM(WIDE, f32)] * count

    def stacked(count):
        return [pltpu.VMEM((2, SLAB_ORBITALS, BLK), f32)] * count

    def slots(count):
        return [pltpu.VMEM((HALF,) + WIDE, f32)] * count

    dma = pltpu.SemaphoreType.DMA
    return pl.pallas_call(
        sweep_kernel,
        out_shape=[shape(WIDE, bf16)] + [shape((2, SLAB_ORBITALS, BLK))] * 2,
        in_specs=[pl.BlockSpec(memory_space=pltpu.SMEM)] * 3 + whole(2) + [pl.BlockSpec(memory_space=pl.ANY)],
        out_specs=whole(3),
        scratch_shapes=[pltpu.VMEM((2, SLAB_ORBITALS, SLAB_ORBITALS), bf16)]
        + [pltpu.VMEM((BW, BW), f32)] * 2
        + slots(3)
        + [pltpu.VMEM((3, 2, SLAB_ORBITALS, BLK), f32)]
        + stacked(6)
        + [
            pltpu.VMEM((3, SLAB_ORBITALS, BW), bf16),
            pltpu.VMEM((PAIRS, 2, BW, BW), f32),
            pltpu.VMEM((2, BW, BW), f32),
        ]
        + slots(2)
        + [pltpu.VMEM((SLAB_ORBITALS, 2 * BW), bf16)]
        + wide(8)
        + [pltpu.VMEM((3, QUARTER, 2 * BW), f32), pltpu.VMEM((QUARTER, 2 * BW), f32)]
        + [dma((3,)), dma((5, 6)), dma((5, 6))]
        + [dma((1, CHUNKS)), dma((1, CHUNKS)), dma((2, CHUNKS)), dma((2, CHUNKS)), dma((6, CHUNKS)), dma((6, CHUNKS))]
        + [dma, dma, dma((7,)), dma((7,))],
        compiler_params=pltpu.CompilerParams(
            collective_id=0, has_side_effects=True, vmem_limit_bytes=VMEM_LIMIT
        ),
    )(shift, weight, index, values, previous, green)


def final_terms(*operands):
    strip = pl.BlockSpec((2, BW, BLK), lambda m: (0, m, 0))
    return pl.pallas_call(
        final_kernel,
        grid=(PAIRS,),
        out_shape=[shape((2, SLAB_ORBITALS, BLK))] * 2,
        in_specs=[
            pl.BlockSpec((2, BW, BW), lambda m: (0, m, PAIRS - 1)),
            pl.BlockSpec(WIDE, lambda m: (0, 0)),
            strip,
            strip,
        ],
        out_specs=[strip, strip],
        compiler_params=pltpu.CompilerParams(vmem_limit_bytes=VMEM_LIMIT),
    )(*operands)


def body(green_ret, prev_lesser, coupling_index, coupling_values, phonon_shift, phonon_weight):
    green = green_ret[0, 0]
    lesser_far, retarded_part, lesser_part = sweep(
        phonon_shift, phonon_weight, coupling_index[0], coupling_values[0], prev_lesser[0, 0], green
    )
    retarded, lesser = final_terms(green, lesser_far, retarded_part, lesser_part)
    return retarded[None, None], lesser[None, None]


def solution(mesh):
    placed = (
        P("slab", "energy", None, None, None),
        P("slab", "energy", None, None, None),
        P("slab", None, None),
        P("slab", None, None, None),
        P(),
        P(),
    )
    return jax.shard_map(
        body,
        mesh=mesh,
        in_specs=placed,
        out_specs=(P("slab", "energy", None, None, None), P("slab", "energy", None, None, None)),
        check_vma=False,
    )
```

```python
import functools

import jax
import jax.numpy as jnp
from jax import lax
from jax.experimental import pallas as pl
from jax.experimental.pallas import tpu as pltpu
from jax.sharding import PartitionSpec as P

SLAB_ORBITALS = 1536
BW = 256
BLK = 128
NBLK = 12
NBW = 2
NMODE = 3
NNZ = 3
PAIRS = SLAB_ORBITALS // BW
HALF = 4

MESH = pl.DeviceIdType.MESH
VMEM_LIMIT = 61 * 1024 * 1024
NN = (((1,), (0,)), ((), ()))
NT = (((1,), (1,)), ((), ()))

f32 = jnp.float32
bf16 = jnp.bfloat16


def dot(left, right, dims=NN):
    return lax.dot_general(left, right, dims, preferred_element_type=f32)


def split(value):
    high = value.astype(bf16)
    return high, (value - high.astype(f32)).astype(bf16)


def turned(value):
    width = value.shape[1] // 2
    return jnp.concatenate([-value[:, width:], value[:, :width]], axis=1)


def doubled(value):
    return jnp.concatenate([value, turned(value)], axis=0)


def product(left, right, dims=NN):
    left_high, left_low = split(left)
    right_high, right_low = split(right)
    main = doubled(right_high)
    return (
        dot(left_high, main, dims) + dot(left_low, main, dims) + dot(left_high, doubled(right_low), dims)
    )


def real_left(matrix, value):
    matrix_high, matrix_low = split(matrix)
    value_high, value_low = split(value)
    return dot(matrix_high, value_high) + dot(matrix_high, value_low) + dot(matrix_low, value_high)


def real_right(value, matrix):
    matrix_high, matrix_low = split(matrix)
    parts = []
    for part in (value[:, :BW], value[:, BW:]):
        high, low = split(part)
        parts.append(dot(high, matrix_high) + dot(low, matrix_high) + dot(high, matrix_low))
    return jnp.concatenate(parts, axis=1)


def beside(ref):
    return jnp.concatenate([ref[0], ref[1]], axis=1)


def adjoint(value):
    return jnp.concatenate([value[:, :BW].T, -value[:, BW:].T], axis=1)


class Place:
    def __init__(self):
        slab, energy = lax.axis_index("slab"), lax.axis_index("energy")
        self.half = slab // HALF
        self.z = slab % HALF
        base = self.half * HALF
        self.right = {"slab": base + (self.z + 1) % HALF}
        self.left = {"slab": base + (self.z + HALF - 1) % HALF}
        self.away = [{"slab": base + (self.z + d) % HALF} for d in (1, 2, 3)]
        other_half = (slab + HALF) % (2 * HALF)
        flipped = energy + 2 - 4 * (energy // 2 % 2)
        self.across = {"slab": other_half}
        self.y_partner = {"energy": flipped}
        self.energy, self.flipped = energy, flipped
        self.core = {"energy": energy + 1 - 2 * (energy % 2)}
        self.x_next = {"energy": (energy + 4) % 16}
        self.x_before = {"energy": (energy + 12) % 16}


def enter(others):
    barrier = pltpu.get_barrier_semaphore()
    for other in others:
        pl.semaphore_signal(barrier, inc=1, device_id=other, device_id_type=MESH)
    pl.semaphore_wait(barrier, len(others))


def sending(source, target, send, recv, device):
    return pltpu.make_async_remote_copy(
        src_ref=source, dst_ref=target, send_sem=send, recv_sem=recv, device_id=device, device_id_type=MESH
    )


class Gather:
    def __init__(self, place, slots, send, recv):
        z = place.z
        low, high = pl.ds(0, BW // 2), pl.ds(BW // 2, BW // 2)
        before, after, opposite = (z + 3) % HALF, (z + 1) % HALF, (z + 2) % HALF

        def copy(index, slot, rows, target):
            part = slots.at[slot, rows]
            return sending(part, part, send.at[index], recv.at[index], target)

        self.first = [
            copy(0, z, low, place.right),
            copy(1, z, high, place.left),
            copy(2, z, high, place.right),
            copy(3, z, low, place.left),
        ]
        self.arrive = [
            copy(0, before, low, place.right),
            copy(1, after, high, place.left),
            copy(2, before, high, place.right),
            copy(3, after, low, place.left),
        ]
        self.relay = [copy(4, before, low, place.right), copy(5, after, high, place.left)]
        self.last = [copy(4, opposite, low, place.right), copy(5, opposite, high, place.left)]

    def start(self):
        for item in self.first:
            item.start()

    def forward(self):
        for index in (0, 1):
            self.arrive[index].wait_recv()
            self.relay[index].start()

    def finish(self):
        for item in self.arrive[2:] + self.last:
            item.wait_recv()
        for item in self.first + self.relay:
            item.wait_send()


CHUNKS = 12
ADD_LAG = 2
USE_LAG = 4
PIECES = 2
ROWS = SLAB_ORBITALS // CHUNKS
QUARTER = BW // HALF
STRIPE = 512


def unit():
    row = lax.broadcasted_iota(jnp.int32, WIDE, 0)
    column = lax.broadcasted_iota(jnp.int32, WIDE, 1)
    return (row == column).astype(f32)


class Shipment:
    def __init__(self, place, term, parts, quarter, total, send, recv):
        z = place.z
        size = QUARTER // PIECES
        pieces = range(PIECES)

        def rows(index, piece):
            return pl.ds(pl.multiple_of((index % HALF) * QUARTER + piece * size, size), size)

        def within(piece):
            return pl.ds(piece * size, size)

        def copy(index, piece, origin, target, device):
            return sending(origin, target, send.at[index, piece], recv.at[index, piece], device)

        def handed(d, piece, index):
            spot = total.at[rows(index, piece)]
            return copy(3 + d, piece, spot, spot, place.away[d - 1])

        self.term, self.parts, self.quarter = term, parts, quarter
        self.here = [rows(z, p) for p in pieces]
        self.within = [within(p) for p in pieces]
        self.spread = [
            [copy(d - 1, p, term.at[rows(z + d, p)], parts.at[d - 1, within(p)], place.away[d - 1]) for d in (1, 2, 3)]
            for p in pieces
        ]
        self.cross = [copy(3, p, quarter.at[within(p)], total.at[rows(z, p)], place.across) for p in pieces]
        self.hand = [[handed(d, p, z) for d in (1, 2, 3)] for p in pieces]
        self.get = [[handed(d, p, z - d) for d in (1, 2, 3)] for p in pieces]

    def start(self):
        for group in self.spread:
            for item in group:
                item.start()

    def pass_over(self):
        for group, here, within, cross in zip(self.spread, self.here, self.within, self.cross):
            for item in group:
                item.wait_recv()
            others = self.parts[0, within, :] + self.parts[1, within, :] + self.parts[2, within, :]
            self.quarter[within, :] = self.term[here, :] + others
            cross.start()

    def hand_on(self):
        for cross, group in zip(self.cross, self.hand):
            cross.wait_recv()
            for item in group:
                item.start()

    def arrive(self):
        for group in self.get:
            for item in group:
                item.wait_recv()

    def sent(self):
        for item in sum(self.spread, self.cross):
            item.wait_send()

    def handed(self):
        for item in sum(self.hand, []):
            item.wait_send()


def partner_weights(target, sources, shift, weight):
    result = []
    for source in sources:
        total = 0.0
        for mode in range(NMODE):
            total = total + jnp.where(source == target + shift[mode], weight[0, mode], 0.0)
            total = total + jnp.where(source == target - shift[mode], weight[1, mode], 0.0)
        result.append(total)
    return result


def dense_coupling(index, values, coupling, coupling_t):
    for row in range(NBW):
        for column in range(NBW):
            block = jnp.zeros((BLK, BLK), f32)
            for item in range(NNZ):
                here = (index[0, item, 0] == row) & (index[0, item, 1] == column)
                block = block + jnp.where(here, 1.0, 0.0) * values[item]
            rows, columns = pl.ds(row * BLK, BLK), pl.ds(column * BLK, BLK)
            coupling[rows, columns] = block
            coupling_t[columns, rows] = block.T


def sweep_kernel(
    shift, weight, index, values, previous, green_hbm,
    lesser_far, retarded_part, lesser_part,
    green, coupling, coupling_t, transfer, inward, corner,
    others, two_away, after, before, passing, from_before, from_after,
    scaled, outer_right, outer_left, source, driven, weighted,
    run, incoming, own, through, term, total, reach, near, parts, quarter, weighting,
    load, z_send, z_recv, y_send, y_recv, core_send, core_recv, x_send, x_recv,
    cross_send, cross_recv, ship_send, ship_recv,
):
    place = Place()
    z, half = place.z, place.half
    steps = range(CHUNKS)
    left, last = pl.ds(0, BW), pl.ds(SLAB_ORBITALS - BW, BW)
    middle = pl.ds(BW, SLAB_ORBITALS - 2 * BW)
    fetch = [
        pltpu.make_async_copy(green_hbm.at[:, span], green.at[:, span], load.at[i])
        for i, span in enumerate((last, left, middle))
    ]
    for item in fetch:
        item.start()
    enter(place.away + [place.across, place.y_partner, place.core, place.x_next, place.x_before])


    def rows(c):
        return pl.ds(c * ROWS, ROWS)

    def part(ref, i):
        return lambda c: ref.at[i, rows(c)]

    def both(ref):
        return lambda c: ref.at[:, rows(c)]

    def copies(sems, kind, origin, target, device):
        send, recv = sems
        return [sending(origin(c), target(c), send.at[kind, c], recv.at[kind, c], device) for c in steps]

    y, core, x = (y_send, y_recv), (core_send, core_recv), (x_send, x_recv)
    over_y = copies(y, 0, both(previous), both(others.at[1]), place.y_partner)
    core_own = copies(core, 0, both(previous), both(others.at[0]), place.core)
    core_more = copies(core, 1, both(others.at[1]), both(others.at[2]), place.core)
    two_low = copies(x, 0, part(two_away, 0), part(passing, 0), place.x_next)
    two_high = copies(x, 1, part(two_away, 1), part(passing, 1), place.x_before)
    after_high = copies(x, 2, part(after, 1), part(from_before, 1), place.x_next)
    before_low = copies(x, 3, part(before, 0), part(from_after, 0), place.x_before)
    after_low = copies(x, 4, part(after, 0), part(from_before, 0), place.x_next)
    before_high = copies(x, 5, part(before, 1), part(from_after, 1), place.x_before)

    over_y[0].start()
    core_own[0].start()

    sources = [place.energy, place.energy + 1 - 2 * (place.energy % 2)]
    sources += [place.flipped, place.flipped + 1 - 2 * (place.flipped % 2)]
    weights = [partner_weights((place.energy + 4 * t) % 16, sources, shift, weight) for t in range(4)]
    dense_coupling(index, values, coupling, coupling_t)
    over_y[1].start()
    core_own[1].start()
    turn = [Gather(place, ref, z_send.at[i], z_recv.at[i]) for i, ref in enumerate((transfer, inward, corner))]

    def near_factors():
        t_high, t_low = split(coupling_t[...])
        fetch[0].wait()
        value = jnp.concatenate([green[0, last, left], green[1, last, left]], axis=1)
        transfer[z] = dot(t_high, value) + dot(t_low, value)
        turn[0].start()
        fetch[1].wait()
        c_high, c_low = split(coupling[...])
        halves = [dot(green[i, left, last], c_high) + dot(green[i, left, last], c_low) for i in (0, 1)]
        inward[z] = jnp.concatenate(halves, axis=1)
        corner[z] = jnp.concatenate([green[0, left, left], green[1, left, left]], axis=1).astype(f32)

    def weigh(c):
        over_y[c].wait_recv()
        core_more[c].start()
        if c + 2 < CHUNKS:
            over_y[c + 2].start()
            core_own[c + 2].start()
        core_own[c].wait_recv()
        core_more[c].wait_recv()
        pieces = [previous[:, rows(c)]] + [others[i, :, rows(c)] for i in (0, 1, 2)]

        def sums(target):
            result = weights[target][0] * pieces[0]
            for i in (1, 2, 3):
                result = result + weights[target][i] * pieces[i]
            return result

        two_away[:, rows(c)] = sums(2)
        two_low[c].start()
        two_high[c].start()
        after[:, rows(c)] = sums(1)
        after_high[c].start()
        before[:, rows(c)] = sums(3)
        before_low[c].start()

    def add_passing(c):
        two_low[c].wait_recv()
        after[0, rows(c)] = after[0, rows(c)] + passing[0, rows(c)]
        after_low[c].start()
        two_high[c].wait_recv()
        before[1, rows(c)] = before[1, rows(c)] + passing[1, rows(c)]
        before_high[c].start()

    def self_energy(c):
        mine = weights[0][0] * previous[:, rows(c)]
        for i in (0, 1, 2):
            mine = mine + weights[0][i + 1] * others[i, :, rows(c)]
        for item in (after_high, before_low, after_low, before_high):
            item[c].wait_recv()
        return (mine + from_before[:, rows(c)] + from_after[:, rows(c)]).astype(bf16)


    def against(values, left_rows, right_rows, columns):
        first = values[0:2, left_rows, :].reshape(2 * BW, BW)
        second = values[1:3, left_rows, :].reshape(2 * BW, BW)
        result = dot(first, green[0, right_rows, columns], NT) + dot(second, green[1, right_rows, columns], NT)
        return result.reshape(2, BW, BW)

    def keep(span, result):
        scaled[0, span[0], span[1]] = result[:, : result.shape[1] // 2]
        scaled[1, span[0], span[1]] = result[:, result.shape[1] // 2 :]
        scaled[2, span[0], span[1]] = -result[:, : result.shape[1] // 2]

    def scale(c):
        sigma = self_energy(c)
        factor = doubled(jnp.concatenate([sigma[0], sigma[1]], axis=1))
        columns = pl.ds(c * BLK, BLK)
        for start in range(0, SLAB_ORBITALS, STRIPE):
            span = pl.ds(start, STRIPE)
            piece = jnp.concatenate([green[0, span, columns], green[1, span, columns]], axis=1)
            keep((span, pl.ds(c % 2 * BLK, BLK)), dot(piece, factor).astype(bf16))

    def last_pair(c):
        far = against(scaled, last, last, pl.ds(c * BW, BW))
        outer_right[PAIRS - 1] = far if c == 0 else outer_right[PAIRS - 1] + far

    def local_terms(c):
        columns = pl.ds(c * BW, BW)

        def pair(m, _):
            span = pl.ds(pl.multiple_of(m * BW, BW), BW)

            @pl.when(m < PAIRS - 1)
            def _():
                far = against(scaled, last, span, columns)
                outer_right[m] = far if c == 0 else outer_right[m] + far

            local = against(scaled, span, span, columns)
            for k in (0, 1):
                block = pl.ds(pl.multiple_of(m * BW + k * BLK, BLK), BLK)
                here = slice(k * BLK, (k + 1) * BLK)
                value = local[:, here, here]
                lesser_part[:, block, :] = value if c == 0 else lesser_part[:, block, :] + value

            @pl.when(m == 0)
            def _():
                outer_left[...] = local if c == 0 else outer_left[...] + local

            return 0

        lax.fori_loop(0, PAIRS, pair, 0)

    def reaches():
        reach[...] = unit()
        near[...] = unit()

        def over_transfer(ref):
            def step(j, _):
                ref[...] = product(transfer[j], ref[...])
                return 0

            return step

        def over_inward(ref):
            def step(i, _):
                j = HALF - 1 - i
                ref[...] = product(inward[j], ref[...])
                return 0

            return step

        @pl.when(half == 0)
        def _():
            lax.fori_loop(z + 1, HALF, over_transfer(reach), 0)
            lax.fori_loop(0, HALF - 1 - z, over_inward(near), 0)

        @pl.when(half == 1)
        def _():
            lax.fori_loop(HALF - z, HALF, over_inward(reach), 0)
            lax.fori_loop(0, z, over_transfer(near), 0)

    near_factors()
    for t in range(CHUNKS + USE_LAG):
        if t < CHUNKS:
            weigh(t)
        if t == USE_LAG:
            fetch[2].wait()
        if t in (2, 6, 10):
            i = (2, 6, 10).index(t)
            turn[i].forward()
            if i < 2:
                turn[i + 1].start()
        if 0 <= t - ADD_LAG < CHUNKS:
            add_passing(t - ADD_LAG)
        if t == CHUNKS + 0:
            turn[0].finish()
            turn[1].finish()
            reaches()
        if t >= USE_LAG:
            scale(t - USE_LAG)
            if (t - USE_LAG) % 2 == 1:
                last_pair((t - USE_LAG) // 2)
                if t < CHUNKS + USE_LAG - 1:
                    local_terms((t - USE_LAG) // 2)


    ship = Shipment(place, term, parts, quarter, total, ship_send, ship_recv)
    over = sending(run, incoming, cross_send, cross_recv, place.across)

    def congruence(factor, value):
        return product(product(factor, value), factor, NT)

    gather = Gather(place, source, z_send.at[3], z_recv.at[3])
    source[z] = real_left(coupling_t[...], real_right(beside(outer_right.at[PAIRS - 1]), coupling[...]))

    @pl.when(half == 0)
    def _():
        term[...] = congruence(reach[...], source[z])
        ship.start()

    gather.start()
    turn[2].finish()

    def retarded_step(i, _):
        j = HALF - 1 - i

        @pl.when(j == z)
        def _():
            own[...] = run[...]

        run[...] = corner[j] + product(product(inward[j], run[...]), transfer[j])
        return 0

    @pl.when(half == 1)
    def _():
        own[...] = jnp.zeros_like(own)
        run[...] = corner[HALF - 1]
        lax.fori_loop(1, HALF, retarded_step, 0)
        over.start()

    local_terms(PAIRS - 1)

    @pl.when(half == 0)
    def _():
        ship.pass_over()

    gather.forward()

    @pl.when(half == 0)
    def _():
        over.wait_recv()
        run[...] = incoming[...]
        lax.fori_loop(0, HALF - 1 - z, retarded_step, 0)
        own[...] = run[...]

    outer = real_right(own[...], coupling_t[...])
    through[...] = product(inward[z], outer)
    weighting[...] = real_left(coupling[...], outer).astype(bf16)

    def use_retarded():
        factor = doubled(weighting[...])
        for start in range(0, SLAB_ORBITALS, STRIPE):
            span = pl.ds(start, STRIPE)
            piece = jnp.concatenate([green[0, span, last], green[1, span, last]], axis=1)
            weighted[span, :] = dot(piece, factor).astype(bf16)

        def pair(m, _):
            span = pl.ds(pl.multiple_of(m * BW, BW), BW)
            result = dot(
                weighted[span, :], doubled(jnp.concatenate([green[0, last, span], green[1, last, span]], axis=1))
            )
            for k in (0, 1):
                block = pl.ds(pl.multiple_of(m * BW + k * BLK, BLK), BLK)
                here = slice(k * BLK, (k + 1) * BLK)
                for i in (0, 1):
                    there = slice(i * BW + k * BLK, i * BW + (k + 1) * BLK)
                    retarded_part[i, block, :] = green[i, block, block].astype(f32) + result[here, there]
            return 0

        lax.fori_loop(0, PAIRS, pair, 0)

    @pl.when(half == 1)
    def _():
        use_retarded()
        ship.hand_on()

    gather.finish()
    own[...] = jnp.zeros_like(own)

    def forward_step(j, _):
        own[...] = congruence(transfer[j], own[...]) + source[j]
        return 0

    @pl.when(z > 0)
    def _():
        own[...] = source[0]

    lax.fori_loop(1, z, forward_step, 0)

    @pl.when(half == 1)
    def _():
        ship.arrive()
        own[...] = own[...] + congruence(near[...], total[...])

    state = doubled(own[...].astype(bf16))
    corner_l = jnp.concatenate([green[0, left, left], green[1, left, left]], axis=1)
    corner_rl = jnp.concatenate([green[0, last, left], green[1, last, left]], axis=1)
    edge = dot(jnp.concatenate([corner_l, corner_rl], axis=0), state).astype(bf16)
    right = dot(edge, doubled(corner_l), NT)
    mixed = product(through[...], beside(outer_right.at[0]) + right[BW:])
    gather = Gather(place, driven, z_send.at[4], z_recv.at[4])
    driven[z] = beside(outer_left) + right[:BW] + mixed + adjoint(mixed)

    gather.start()

    @pl.when(half == 1)
    def _():
        term[...] = congruence(reach[...], driven[z])
        ship.start()

    gather.forward()

    @pl.when(half == 1)
    def _():
        ship.pass_over()

    @pl.when(half == 0)
    def _():
        use_retarded()

    for start in range(0, SLAB_ORBITALS, STRIPE):
        span = pl.ds(start, STRIPE)
        piece = jnp.concatenate([green[0, span, left], green[1, span, left]], axis=1)
        keep((span, pl.ds(0, BW)), dot(piece, state).astype(bf16))

    def pair(m, _):
        span = pl.ds(pl.multiple_of(m * BW, BW), BW)
        far_right = (outer_right[m] + against(scaled, last, span, left)).astype(bf16)
        mixed = dot(weighted[span, :], doubled(jnp.concatenate([far_right[0], far_right[1]], axis=1)))
        local = against(scaled, span, span, left)
        for k in (0, 1):
            block = pl.ds(pl.multiple_of(m * BW + k * BLK, BLK), BLK)
            here = slice(k * BLK, (k + 1) * BLK)
            for i in (0, 1):
                there = slice(i * BW + k * BLK, i * BW + (k + 1) * BLK)
                mix = mixed[here, there]
                mirrored = mix.T if i == 0 else -mix.T
                lesser_part[i, block, :] = lesser_part[i, block, :] + local[i, here, here] + mix + mirrored
        return 0

    lax.fori_loop(0, PAIRS, pair, 0)

    @pl.when(half == 0)
    def _():
        ship.hand_on()

    gather.finish()
    own[...] = jnp.zeros_like(own)

    def backward_step(i, _):
        j = HALF - 1 - i
        own[...] = congruence(inward[j], own[...]) + driven[j]
        return 0

    @pl.when(z < HALF - 1)
    def _():
        own[...] = driven[HALF - 1]

    lax.fori_loop(1, HALF - 1 - z, backward_step, 0)

    @pl.when(half == 0)
    def _():
        ship.arrive()
        own[...] = own[...] + congruence(near[...], total[...])

    lesser_far[...] = real_left(coupling[...], real_right(own[...], coupling_t[...])).astype(bf16)
    ship.sent()
    ship.handed()

    @pl.when(half == 1)
    def _():
        over.wait_send()

    for group in (
        over_y, core_own, core_more, two_low, two_high, after_high, before_low, after_low, before_high,
    ):
        for item in group:
            item.wait_send()


def final_kernel(green, lesser_far, retarded_part, lesser_part, retarded_out, lesser_out):
    factor = doubled(lesser_far[...])
    retarded_out[...] = retarded_part[...]
    for start in range(0, STRIPE, BW):
        span = slice(start, start + BW)
        right = jnp.concatenate([green[0, span], green[1, span]], axis=1)
        weighted = dot(right, factor).astype(bf16)
        real, imag = weighted[:, :BW], weighted[:, BW:]
        first = jnp.concatenate([real, imag], axis=0)
        second = jnp.concatenate([imag, -real], axis=0)
        total = dot(first, green[0, span], NT) + dot(second, green[1, span], NT)
        for k in (0, 1):
            block = slice(k * BLK, (k + 1) * BLK)
            rows = slice(start + k * BLK, start + (k + 1) * BLK)
            for i in (0, 1):
                here = slice(i * BW + k * BLK, i * BW + (k + 1) * BLK)
                lesser_out[i, rows, :] = lesser_part[i, rows, :] + total[here, block]


def whole(count):
    return [pl.BlockSpec(memory_space=pltpu.VMEM)] * count


def shape(dims, dtype=f32):
    return jax.ShapeDtypeStruct(dims, dtype)


WIDE = (BW, 2 * BW)


def sweep(shift, weight, index, values, previous, green):
    def wide(count):
        return [pltpu.VMEM(WIDE, f32)] * count

    def stacked(count):
        return [pltpu.VMEM((2, SLAB_ORBITALS, BLK), f32)] * count

    def slots(count):
        return [pltpu.VMEM((HALF,) + WIDE, f32)] * count

    dma = pltpu.SemaphoreType.DMA
    return pl.pallas_call(
        sweep_kernel,
        out_shape=[shape(WIDE, bf16)] + [shape((2, SLAB_ORBITALS, BLK))] * 2,
        in_specs=[pl.BlockSpec(memory_space=pltpu.SMEM)] * 3 + whole(2) + [pl.BlockSpec(memory_space=pl.ANY)],
        out_specs=whole(3),
        scratch_shapes=[pltpu.VMEM((2, SLAB_ORBITALS, SLAB_ORBITALS), bf16)]
        + [pltpu.VMEM((BW, BW), f32)] * 2
        + slots(3)
        + [pltpu.VMEM((3, 2, SLAB_ORBITALS, BLK), f32)]
        + stacked(6)
        + [
            pltpu.VMEM((3, SLAB_ORBITALS, BW), bf16),
            pltpu.VMEM((PAIRS, 2, BW, BW), f32),
            pltpu.VMEM((2, BW, BW), f32),
        ]
        + slots(2)
        + [pltpu.VMEM((SLAB_ORBITALS, 2 * BW), bf16)]
        + wide(8)
        + [pltpu.VMEM((3, QUARTER, 2 * BW), f32), pltpu.VMEM((QUARTER, 2 * BW), f32), pltpu.VMEM(WIDE, bf16)]
        + [dma((3,)), dma((5, 6)), dma((5, 6))]
        + [dma((1, CHUNKS)), dma((1, CHUNKS)), dma((2, CHUNKS)), dma((2, CHUNKS)), dma((6, CHUNKS)), dma((6, CHUNKS))]
        + [dma, dma, dma((7, PIECES)), dma((7, PIECES))],
        compiler_params=pltpu.CompilerParams(
            collective_id=0, has_side_effects=True, vmem_limit_bytes=VMEM_LIMIT
        ),
    )(shift, weight, index, values, previous, green)


def final_terms(*operands):
    strip = pl.BlockSpec((2, STRIPE, BLK), lambda m: (0, m, 0))
    return pl.pallas_call(
        final_kernel,
        grid=(SLAB_ORBITALS // STRIPE,),
        out_shape=[shape((2, SLAB_ORBITALS, BLK))] * 2,
        in_specs=[
            pl.BlockSpec((2, STRIPE, BW), lambda m: (0, m, PAIRS - 1)),
            pl.BlockSpec(WIDE, lambda m: (0, 0)),
            strip,
            strip,
        ],
        out_specs=[strip, strip],
        compiler_params=pltpu.CompilerParams(vmem_limit_bytes=VMEM_LIMIT),
    )(*operands)


def body(green_ret, prev_lesser, coupling_index, coupling_values, phonon_shift, phonon_weight):
    green = green_ret[0, 0]
    lesser_far, retarded_part, lesser_part = sweep(
        phonon_shift, phonon_weight, coupling_index, coupling_values[0], prev_lesser[0, 0], green
    )
    retarded, lesser = final_terms(green, lesser_far, retarded_part, lesser_part)
    return retarded[None, None], lesser[None, None]


def solution(mesh):
    placed = (
        P("slab", "energy", None, None, None),
        P("slab", "energy", None, None, None),
        P("slab", None, None),
        P("slab", None, None, None),
        P(),
        P(),
    )
    return jax.shard_map(
        body,
        mesh=mesh,
        in_specs=placed,
        out_specs=(P("slab", "energy", None, None, None), P("slab", "energy", None, None, None)),
        check_vma=False,
    )
```

```python
import functools

import jax
import jax.numpy as jnp
from jax import lax
from jax.experimental import pallas as pl
from jax.experimental.pallas import tpu as pltpu
from jax.sharding import PartitionSpec as P

SLAB_ORBITALS = 1536
BW = 256
BLK = 128
NBLK = 12
NBW = 2
NMODE = 3
NNZ = 3
PAIRS = SLAB_ORBITALS // BW
HALF = 4

MESH = pl.DeviceIdType.MESH
VMEM_LIMIT = 61 * 1024 * 1024
NN = (((1,), (0,)), ((), ()))
NT = (((1,), (1,)), ((), ()))

f32 = jnp.float32
bf16 = jnp.bfloat16


def dot(left, right, dims=NN):
    return lax.dot_general(left, right, dims, preferred_element_type=f32)


def split(value):
    high = value.astype(bf16)
    return high, (value - high.astype(f32)).astype(bf16)


def turned(value):
    width = value.shape[1] // 2
    return jnp.concatenate([-value[:, width:], value[:, :width]], axis=1)


def doubled(value):
    return jnp.concatenate([value, turned(value)], axis=0)


def product(left, right, dims=NN):
    left_high, left_low = split(left)
    right_high, right_low = split(right)
    main = doubled(right_high)
    return (
        dot(left_high, main, dims) + dot(left_low, main, dims) + dot(left_high, doubled(right_low), dims)
    )


def real_left(matrix, value):
    matrix_high, matrix_low = split(matrix)
    value_high, value_low = split(value)
    return dot(matrix_high, value_high) + dot(matrix_high, value_low) + dot(matrix_low, value_high)


def real_right(value, matrix):
    matrix_high, matrix_low = split(matrix)
    parts = []
    for part in (value[:, :BW], value[:, BW:]):
        high, low = split(part)
        parts.append(dot(high, matrix_high) + dot(low, matrix_high) + dot(high, matrix_low))
    return jnp.concatenate(parts, axis=1)


def beside(ref):
    return jnp.concatenate([ref[0], ref[1]], axis=1)


def adjoint(value):
    return jnp.concatenate([value[:, :BW].T, -value[:, BW:].T], axis=1)


class Place:
    def __init__(self):
        slab, energy = lax.axis_index("slab"), lax.axis_index("energy")
        self.half = slab // HALF
        self.z = slab % HALF
        base = self.half * HALF
        self.right = {"slab": base + (self.z + 1) % HALF}
        self.left = {"slab": base + (self.z + HALF - 1) % HALF}
        self.away = [{"slab": base + (self.z + d) % HALF} for d in (1, 2, 3)]
        other_half = (slab + HALF) % (2 * HALF)
        flipped = energy + 2 - 4 * (energy // 2 % 2)
        self.across = {"slab": other_half}
        self.y_partner = {"energy": flipped}
        self.energy, self.flipped = energy, flipped
        self.core = {"energy": energy + 1 - 2 * (energy % 2)}
        self.x_next = {"energy": (energy + 4) % 16}
        self.x_before = {"energy": (energy + 12) % 16}


def enter(others):
    barrier = pltpu.get_barrier_semaphore()
    for other in others:
        pl.semaphore_signal(barrier, inc=1, device_id=other, device_id_type=MESH)
    pl.semaphore_wait(barrier, len(others))


def sending(source, target, send, recv, device):
    return pltpu.make_async_remote_copy(
        src_ref=source, dst_ref=target, send_sem=send, recv_sem=recv, device_id=device, device_id_type=MESH
    )


class Gather:
    def __init__(self, place, slots, send, recv):
        z = place.z
        low, high = pl.ds(0, BW // 2), pl.ds(BW // 2, BW // 2)
        before, after, opposite = (z + 3) % HALF, (z + 1) % HALF, (z + 2) % HALF

        def copy(index, slot, rows, target):
            part = slots.at[slot, rows]
            return sending(part, part, send.at[index], recv.at[index], target)

        self.first = [
            copy(0, z, low, place.right),
            copy(1, z, high, place.left),
            copy(2, z, high, place.right),
            copy(3, z, low, place.left),
        ]
        self.arrive = [
            copy(0, before, low, place.right),
            copy(1, after, high, place.left),
            copy(2, before, high, place.right),
            copy(3, after, low, place.left),
        ]
        self.relay = [copy(4, before, low, place.right), copy(5, after, high, place.left)]
        self.last = [copy(4, opposite, low, place.right), copy(5, opposite, high, place.left)]

    def start(self):
        for item in self.first:
            item.start()

    def forward(self):
        for index in (0, 1):
            self.arrive[index].wait_recv()
            self.relay[index].start()

    def finish(self):
        for item in self.arrive[2:] + self.last:
            item.wait_recv()
        for item in self.first + self.relay:
            item.wait_send()


CHUNKS = 12
ADD_LAG = 2
USE_LAG = 4
PIECES = 2
ROWS = SLAB_ORBITALS // CHUNKS
QUARTER = BW // HALF
STRIPE = 512


def unit():
    row = lax.broadcasted_iota(jnp.int32, WIDE, 0)
    column = lax.broadcasted_iota(jnp.int32, WIDE, 1)
    return (row == column).astype(f32)


class Shipment:
    def __init__(self, place, term, parts, quarter, total, send, recv):
        z = place.z
        size = QUARTER // PIECES
        pieces = range(PIECES)

        def rows(index, piece):
            return pl.ds(pl.multiple_of((index % HALF) * QUARTER + piece * size, size), size)

        def within(piece):
            return pl.ds(piece * size, size)

        def copy(index, piece, origin, target, device):
            return sending(origin, target, send.at[index, piece], recv.at[index, piece], device)

        def handed(d, piece, index):
            spot = total.at[rows(index, piece)]
            return copy(3 + d, piece, spot, spot, place.away[d - 1])

        self.term, self.parts, self.quarter = term, parts, quarter
        self.here = [rows(z, p) for p in pieces]
        self.within = [within(p) for p in pieces]
        self.spread = [
            [copy(d - 1, p, term.at[rows(z + d, p)], parts.at[d - 1, within(p)], place.away[d - 1]) for d in (1, 2, 3)]
            for p in pieces
        ]
        self.cross = [copy(3, p, quarter.at[within(p)], total.at[rows(z, p)], place.across) for p in pieces]
        self.hand = [[handed(d, p, z) for d in (1, 2, 3)] for p in pieces]
        self.get = [[handed(d, p, z - d) for d in (1, 2, 3)] for p in pieces]

    def start(self):
        for group in self.spread:
            for item in group:
                item.start()

    def pass_over(self):
        for group, here, within, cross in zip(self.spread, self.here, self.within, self.cross):
            for item in group:
                item.wait_recv()
            others = self.parts[0, within, :] + self.parts[1, within, :] + self.parts[2, within, :]
            self.quarter[within, :] = self.term[here, :] + others
            cross.start()

    def hand_on(self):
        for cross, group in zip(self.cross, self.hand):
            cross.wait_recv()
            for item in group:
                item.start()

    def arrive(self):
        for group in self.get:
            for item in group:
                item.wait_recv()

    def sent(self):
        for item in sum(self.spread, self.cross):
            item.wait_send()

    def handed(self):
        for item in sum(self.hand, []):
            item.wait_send()


def partner_weights(target, sources, shift, weight):
    result = []
    for source in sources:
        total = 0.0
        for mode in range(NMODE):
            total = total + jnp.where(source == target + shift[mode], weight[0, mode], 0.0)
            total = total + jnp.where(source == target - shift[mode], weight[1, mode], 0.0)
        result.append(total)
    return result


def dense_coupling(index, values, coupling, coupling_t):
    for row in range(NBW):
        for column in range(NBW):
            block = jnp.zeros((BLK, BLK), f32)
            for item in range(NNZ):
                here = (index[0, 0, item] == row) & (index[0, 1, item] == column)
                block = block + jnp.where(here, 1.0, 0.0) * values[item]
            rows, columns = pl.ds(row * BLK, BLK), pl.ds(column * BLK, BLK)
            coupling[rows, columns] = block
            coupling_t[columns, rows] = block.T


def sweep_kernel(
    shift, weight, index, values, previous, green_hbm,
    lesser_far, retarded_part, lesser_part,
    green, coupling, coupling_t, transfer, inward, corner,
    others, two_away, after, before, passing, from_before, from_after,
    scaled, outer_right, outer_left, source, driven, weighted,
    run, incoming, own, through, term, total, reach, near, parts, quarter, weighting,
    load, z_send, z_recv, y_send, y_recv, core_send, core_recv, x_send, x_recv,
    cross_send, cross_recv, ship_send, ship_recv,
):
    place = Place()
    z, half = place.z, place.half
    steps = range(CHUNKS)
    left, last = pl.ds(0, BW), pl.ds(SLAB_ORBITALS - BW, BW)
    middle = pl.ds(BW, SLAB_ORBITALS - 2 * BW)
    fetch = [
        pltpu.make_async_copy(green_hbm.at[:, span], green.at[:, span], load.at[i])
        for i, span in enumerate((last, left, middle))
    ]
    for item in fetch:
        item.start()
    enter(place.away + [place.across, place.y_partner, place.core, place.x_next, place.x_before])


    def rows(c):
        return pl.ds(c * ROWS, ROWS)

    def part(ref, i):
        return lambda c: ref.at[i, rows(c)]

    def both(ref):
        return lambda c: ref.at[:, rows(c)]

    def copies(sems, kind, origin, target, device):
        send, recv = sems
        return [sending(origin(c), target(c), send.at[kind, c], recv.at[kind, c], device) for c in steps]

    y, core, x = (y_send, y_recv), (core_send, core_recv), (x_send, x_recv)
    over_y = copies(y, 0, both(previous), both(others.at[1]), place.y_partner)
    core_own = copies(core, 0, both(previous), both(others.at[0]), place.core)
    core_more = copies(core, 1, both(others.at[1]), both(others.at[2]), place.core)
    two_low = copies(x, 0, part(two_away, 0), part(passing, 0), place.x_next)
    two_high = copies(x, 1, part(two_away, 1), part(passing, 1), place.x_before)
    after_high = copies(x, 2, part(after, 1), part(from_before, 1), place.x_next)
    before_low = copies(x, 3, part(before, 0), part(from_after, 0), place.x_before)
    after_low = copies(x, 4, part(after, 0), part(from_before, 0), place.x_next)
    before_high = copies(x, 5, part(before, 1), part(from_after, 1), place.x_before)

    over_y[0].start()
    core_own[0].start()

    sources = [place.energy, place.energy + 1 - 2 * (place.energy % 2)]
    sources += [place.flipped, place.flipped + 1 - 2 * (place.flipped % 2)]
    weights = [partner_weights((place.energy + 4 * t) % 16, sources, shift, weight) for t in range(4)]
    dense_coupling(index, values, coupling, coupling_t)
    over_y[1].start()
    core_own[1].start()
    turn = [Gather(place, ref, z_send.at[i], z_recv.at[i]) for i, ref in enumerate((transfer, inward, corner))]

    def near_factors():
        t_high, t_low = split(coupling_t[...])
        fetch[0].wait()
        value = jnp.concatenate([green[0, last, left], green[1, last, left]], axis=1)
        transfer[z] = dot(t_high, value) + dot(t_low, value)
        turn[0].start()
        fetch[1].wait()
        c_high, c_low = split(coupling[...])
        halves = [dot(green[i, left, last], c_high) + dot(green[i, left, last], c_low) for i in (0, 1)]
        inward[z] = jnp.concatenate(halves, axis=1)
        corner[z] = jnp.concatenate([green[0, left, left], green[1, left, left]], axis=1).astype(f32)

    def weigh(c):
        over_y[c].wait_recv()
        core_more[c].start()
        if c + 2 < CHUNKS:
            over_y[c + 2].start()
            core_own[c + 2].start()
        core_own[c].wait_recv()
        core_more[c].wait_recv()
        pieces = [previous[:, rows(c)]] + [others[i, :, rows(c)] for i in (0, 1, 2)]

        def sums(target):
            result = weights[target][0] * pieces[0]
            for i in (1, 2, 3):
                result = result + weights[target][i] * pieces[i]
            return result

        two_away[:, rows(c)] = sums(2)
        two_low[c].start()
        two_high[c].start()
        after[:, rows(c)] = sums(1)
        after_high[c].start()
        before[:, rows(c)] = sums(3)
        before_low[c].start()

    def add_passing(c):
        two_low[c].wait_recv()
        after[0, rows(c)] = after[0, rows(c)] + passing[0, rows(c)]
        after_low[c].start()
        two_high[c].wait_recv()
        before[1, rows(c)] = before[1, rows(c)] + passing[1, rows(c)]
        before_high[c].start()

    def self_energy(c):
        mine = weights[0][0] * previous[:, rows(c)]
        for i in (0, 1, 2):
            mine = mine + weights[0][i + 1] * others[i, :, rows(c)]
        for item in (after_high, before_low, after_low, before_high):
            item[c].wait_recv()
        return (mine + from_before[:, rows(c)] + from_after[:, rows(c)]).astype(bf16)


    def against(values, left_rows, right_rows, columns):
        first = values[0:2, left_rows, :].reshape(2 * BW, BW)
        second = values[1:3, left_rows, :].reshape(2 * BW, BW)
        result = dot(first, green[0, right_rows, columns], NT) + dot(second, green[1, right_rows, columns], NT)
        return result.reshape(2, BW, BW)

    def keep(span, result):
        scaled[0, span[0], span[1]] = result[:, : result.shape[1] // 2]
        scaled[1, span[0], span[1]] = result[:, result.shape[1] // 2 :]
        scaled[2, span[0], span[1]] = -result[:, : result.shape[1] // 2]

    def scale(c):
        sigma = self_energy(c)
        factor = doubled(jnp.concatenate([sigma[0], sigma[1]], axis=1))
        columns = pl.ds(c * BLK, BLK)
        for start in range(0, SLAB_ORBITALS, STRIPE):
            span = pl.ds(start, STRIPE)
            piece = jnp.concatenate([green[0, span, columns], green[1, span, columns]], axis=1)
            keep((span, pl.ds(c % 2 * BLK, BLK)), dot(piece, factor).astype(bf16))

    def last_pair(c):
        far = against(scaled, last, last, pl.ds(c * BW, BW))
        outer_right[PAIRS - 1] = far if c == 0 else outer_right[PAIRS - 1] + far

    def local_terms(c):
        columns = pl.ds(c * BW, BW)

        def pair(m, _):
            span = pl.ds(pl.multiple_of(m * BW, BW), BW)

            @pl.when(m < PAIRS - 1)
            def _():
                far = against(scaled, last, span, columns)
                outer_right[m] = far if c == 0 else outer_right[m] + far

            local = against(scaled, span, span, columns)
            for k in (0, 1):
                block = pl.ds(pl.multiple_of(m * BW + k * BLK, BLK), BLK)
                here = slice(k * BLK, (k + 1) * BLK)
                value = local[:, here, here]
                lesser_part[:, block, :] = value if c == 0 else lesser_part[:, block, :] + value

            @pl.when(m == 0)
            def _():
                outer_left[...] = local if c == 0 else outer_left[...] + local

            return 0

        lax.fori_loop(0, PAIRS, pair, 0)

    def reaches():
        reach[...] = unit()
        near[...] = unit()

        def over_transfer(ref):
            def step(j, _):
                ref[...] = product(transfer[j], ref[...])
                return 0

            return step

        def over_inward(ref):
            def step(i, _):
                j = HALF - 1 - i
                ref[...] = product(inward[j], ref[...])
                return 0

            return step

        @pl.when(half == 0)
        def _():
            lax.fori_loop(z + 1, HALF, over_transfer(reach), 0)
            lax.fori_loop(0, HALF - 1 - z, over_inward(near), 0)

        @pl.when(half == 1)
        def _():
            lax.fori_loop(HALF - z, HALF, over_inward(reach), 0)
            lax.fori_loop(0, z, over_transfer(near), 0)

    near_factors()
    for t in range(CHUNKS + USE_LAG):
        if t < CHUNKS:
            weigh(t)
        if t == USE_LAG:
            fetch[2].wait()
        if t in (2, 6, 10):
            i = (2, 6, 10).index(t)
            turn[i].forward()
            if i < 2:
                turn[i + 1].start()
        if 0 <= t - ADD_LAG < CHUNKS:
            add_passing(t - ADD_LAG)
        if t == CHUNKS + 0:
            turn[0].finish()
            turn[1].finish()
            reaches()
        if t >= USE_LAG:
            scale(t - USE_LAG)
            if (t - USE_LAG) % 2 == 1:
                last_pair((t - USE_LAG) // 2)
                if t < CHUNKS + USE_LAG - 1:
                    local_terms((t - USE_LAG) // 2)


    ship = Shipment(place, term, parts, quarter, total, ship_send, ship_recv)
    over = sending(run, incoming, cross_send, cross_recv, place.across)

    def congruence(factor, value):
        return product(product(factor, value), factor, NT)

    gather = Gather(place, source, z_send.at[3], z_recv.at[3])
    source[z] = real_left(coupling_t[...], real_right(beside(outer_right.at[PAIRS - 1]), coupling[...]))

    @pl.when(half == 0)
    def _():
        term[...] = congruence(reach[...], source[z])
        ship.start()

    gather.start()
    turn[2].finish()

    def retarded_step(i, _):
        j = HALF - 1 - i

        @pl.when(j == z)
        def _():
            own[...] = run[...]

        run[...] = corner[j] + product(product(inward[j], run[...]), transfer[j])
        return 0

    @pl.when(half == 1)
    def _():
        own[...] = jnp.zeros_like(own)
        run[...] = corner[HALF - 1]
        lax.fori_loop(1, HALF, retarded_step, 0)
        over.start()

    local_terms(PAIRS - 1)

    @pl.when(half == 0)
    def _():
        ship.pass_over()

    gather.forward()

    @pl.when(half == 0)
    def _():
        over.wait_recv()
        run[...] = incoming[...]
        lax.fori_loop(0, HALF - 1 - z, retarded_step, 0)
        own[...] = run[...]

    outer = real_right(own[...], coupling_t[...])
    through[...] = product(inward[z], outer)
    weighting[...] = real_left(coupling[...], outer).astype(bf16)

    def use_retarded():
        factor = doubled(weighting[...])
        for start in range(0, SLAB_ORBITALS, STRIPE):
            span = pl.ds(start, STRIPE)
            piece = jnp.concatenate([green[0, span, last], green[1, span, last]], axis=1)
            weighted[span, :] = dot(piece, factor).astype(bf16)

        def pair(m, _):
            span = pl.ds(pl.multiple_of(m * BW, BW), BW)
            result = dot(
                weighted[span, :], doubled(jnp.concatenate([green[0, last, span], green[1, last, span]], axis=1))
            )
            for k in (0, 1):
                block = pl.ds(pl.multiple_of(m * BW + k * BLK, BLK), BLK)
                here = slice(k * BLK, (k + 1) * BLK)
                for i in (0, 1):
                    there = slice(i * BW + k * BLK, i * BW + (k + 1) * BLK)
                    retarded_part[i, block, :] = green[i, block, block].astype(f32) + result[here, there]
            return 0

        lax.fori_loop(0, PAIRS, pair, 0)

    @pl.when(half == 1)
    def _():
        use_retarded()
        ship.hand_on()

    gather.finish()
    own[...] = jnp.zeros_like(own)

    def forward_step(j, _):
        own[...] = congruence(transfer[j], own[...]) + source[j]
        return 0

    @pl.when(z > 0)
    def _():
        own[...] = source[0]

    lax.fori_loop(1, z, forward_step, 0)

    @pl.when(half == 1)
    def _():
        ship.arrive()
        own[...] = own[...] + congruence(near[...], total[...])

    state = doubled(own[...].astype(bf16))
    corner_l = jnp.concatenate([green[0, left, left], green[1, left, left]], axis=1)
    corner_rl = jnp.concatenate([green[0, last, left], green[1, last, left]], axis=1)
    edge = dot(jnp.concatenate([corner_l, corner_rl], axis=0), state).astype(bf16)
    right = dot(edge, doubled(corner_l), NT)
    mixed = product(through[...], beside(outer_right.at[0]) + right[BW:])
    gather = Gather(place, driven, z_send.at[4], z_recv.at[4])
    driven[z] = beside(outer_left) + right[:BW] + mixed + adjoint(mixed)

    gather.start()

    @pl.when(half == 1)
    def _():
        term[...] = congruence(reach[...], driven[z])
        ship.start()

    gather.forward()

    @pl.when(half == 1)
    def _():
        ship.pass_over()

    @pl.when(half == 0)
    def _():
        use_retarded()

    for start in range(0, SLAB_ORBITALS, STRIPE):
        span = pl.ds(start, STRIPE)
        piece = jnp.concatenate([green[0, span, left], green[1, span, left]], axis=1)
        keep((span, pl.ds(0, BW)), dot(piece, state).astype(bf16))

    def pair(m, _):
        span = pl.ds(pl.multiple_of(m * BW, BW), BW)
        far_right = (outer_right[m] + against(scaled, last, span, left)).astype(bf16)
        mixed = dot(weighted[span, :], doubled(jnp.concatenate([far_right[0], far_right[1]], axis=1)))
        local = against(scaled, span, span, left)
        for k in (0, 1):
            block = pl.ds(pl.multiple_of(m * BW + k * BLK, BLK), BLK)
            here = slice(k * BLK, (k + 1) * BLK)
            for i in (0, 1):
                there = slice(i * BW + k * BLK, i * BW + (k + 1) * BLK)
                mix = mixed[here, there]
                mirrored = mix.T if i == 0 else -mix.T
                lesser_part[i, block, :] = lesser_part[i, block, :] + local[i, here, here] + mix + mirrored
        return 0

    lax.fori_loop(0, PAIRS, pair, 0)

    @pl.when(half == 0)
    def _():
        ship.hand_on()

    gather.finish()
    own[...] = jnp.zeros_like(own)

    def backward_step(i, _):
        j = HALF - 1 - i
        own[...] = congruence(inward[j], own[...]) + driven[j]
        return 0

    @pl.when(z < HALF - 1)
    def _():
        own[...] = driven[HALF - 1]

    lax.fori_loop(1, HALF - 1 - z, backward_step, 0)

    @pl.when(half == 0)
    def _():
        ship.arrive()
        own[...] = own[...] + congruence(near[...], total[...])

    lesser_far[...] = real_left(coupling[...], real_right(own[...], coupling_t[...])).astype(bf16)
    ship.sent()
    ship.handed()

    @pl.when(half == 1)
    def _():
        over.wait_send()

    for group in (
        over_y, core_own, core_more, two_low, two_high, after_high, before_low, after_low, before_high,
    ):
        for item in group:
            item.wait_send()


def final_kernel(green, lesser_far, retarded_part, lesser_part, retarded_out, lesser_out):
    factor = doubled(lesser_far[...])
    retarded_out[...] = retarded_part[...]
    for start in range(0, STRIPE, BW):
        span = slice(start, start + BW)
        right = jnp.concatenate([green[0, span], green[1, span]], axis=1)
        weighted = dot(right, factor).astype(bf16)
        real, imag = weighted[:, :BW], weighted[:, BW:]
        first = jnp.concatenate([real, imag], axis=0)
        second = jnp.concatenate([imag, -real], axis=0)
        total = dot(first, green[0, span], NT) + dot(second, green[1, span], NT)
        for k in (0, 1):
            block = slice(k * BLK, (k + 1) * BLK)
            rows = slice(start + k * BLK, start + (k + 1) * BLK)
            for i in (0, 1):
                here = slice(i * BW + k * BLK, i * BW + (k + 1) * BLK)
                lesser_out[i, rows, :] = lesser_part[i, rows, :] + total[here, block]


def whole(count):
    return [pl.BlockSpec(memory_space=pltpu.VMEM)] * count


def shape(dims, dtype=f32):
    return jax.ShapeDtypeStruct(dims, dtype)


WIDE = (BW, 2 * BW)


def sweep(shift, weight, index, values, previous, green):
    def wide(count):
        return [pltpu.VMEM(WIDE, f32)] * count

    def stacked(count):
        return [pltpu.VMEM((2, SLAB_ORBITALS, BLK), f32)] * count

    def slots(count):
        return [pltpu.VMEM((HALF,) + WIDE, f32)] * count

    dma = pltpu.SemaphoreType.DMA
    return pl.pallas_call(
        sweep_kernel,
        out_shape=[shape(WIDE, bf16)] + [shape((2, SLAB_ORBITALS, BLK))] * 2,
        in_specs=[pl.BlockSpec(memory_space=pltpu.SMEM)] * 3 + whole(2) + [pl.BlockSpec(memory_space=pl.ANY)],
        out_specs=whole(3),
        scratch_shapes=[pltpu.VMEM((2, SLAB_ORBITALS, SLAB_ORBITALS), bf16)]
        + [pltpu.VMEM((BW, BW), f32)] * 2
        + slots(3)
        + [pltpu.VMEM((3, 2, SLAB_ORBITALS, BLK), f32)]
        + stacked(6)
        + [
            pltpu.VMEM((3, SLAB_ORBITALS, BW), bf16),
            pltpu.VMEM((PAIRS, 2, BW, BW), f32),
            pltpu.VMEM((2, BW, BW), f32),
        ]
        + slots(2)
        + [pltpu.VMEM((SLAB_ORBITALS, 2 * BW), bf16)]
        + wide(8)
        + [pltpu.VMEM((3, QUARTER, 2 * BW), f32), pltpu.VMEM((QUARTER, 2 * BW), f32), pltpu.VMEM(WIDE, bf16)]
        + [dma((3,)), dma((5, 6)), dma((5, 6))]
        + [dma((1, CHUNKS)), dma((1, CHUNKS)), dma((2, CHUNKS)), dma((2, CHUNKS)), dma((6, CHUNKS)), dma((6, CHUNKS))]
        + [dma, dma, dma((7, PIECES)), dma((7, PIECES))],
        compiler_params=pltpu.CompilerParams(
            collective_id=0, has_side_effects=True, vmem_limit_bytes=VMEM_LIMIT
        ),
    )(shift, weight, index, values, previous, green)


def final_terms(*operands):
    strip = pl.BlockSpec((2, STRIPE, BLK), lambda m: (0, m, 0))
    return pl.pallas_call(
        final_kernel,
        grid=(SLAB_ORBITALS // STRIPE,),
        out_shape=[shape((2, SLAB_ORBITALS, BLK))] * 2,
        in_specs=[
            pl.BlockSpec((2, STRIPE, BW), lambda m: (0, m, PAIRS - 1)),
            pl.BlockSpec(WIDE, lambda m: (0, 0)),
            strip,
            strip,
        ],
        out_specs=[strip, strip],
        compiler_params=pltpu.CompilerParams(vmem_limit_bytes=VMEM_LIMIT),
    )(*operands)


def body(green_ret, prev_lesser, coupling_index, coupling_values, phonon_shift, phonon_weight):
    green = green_ret[0, 0]
    lesser_far, retarded_part, lesser_part = sweep(
        phonon_shift, phonon_weight, jnp.swapaxes(coupling_index, 1, 2), coupling_values[0], prev_lesser[0, 0], green
    )
    retarded, lesser = final_terms(green, lesser_far, retarded_part, lesser_part)
    return retarded[None, None], lesser[None, None]


def solution(mesh):
    placed = (
        P("slab", "energy", None, None, None),
        P("slab", "energy", None, None, None),
        P("slab", None, None),
        P("slab", None, None, None),
        P(),
        P(),
    )
    return jax.shard_map(
        body,
        mesh=mesh,
        in_specs=placed,
        out_specs=(P("slab", "energy", None, None, None), P("slab", "energy", None, None, None)),
        check_vma=False,
    )
```
